256 devices in a mesh: ex: 32 (over y, z), lay: 8 (over x, core).
Axes of the slice: x: 4, y: 4, z: 8, core: 2. Of those that a mesh axis runs over, the one named last changes fastest.
Arguments:
- acts: bfloat16 [65536, 5120], P('ex', 'lay'), may hold values from -6 to 6
- grads: bfloat16 [65536, 13824], P('ex', 'lay'), may hold values from -6 to 6
- act_basis: bfloat16 [5120, 5120], P('lay', 'ex'), may hold values from -0.078125 to 0.078125
- grad_basis: bfloat16 [13824, 13824], P('lay', 'ex'), may hold values from -0.0546875 to 0.0546875
- act_query: bfloat16 [5120, 512], P('ex'), may hold values from -0.078125 to 0.078125
- grad_query: bfloat16 [13824, 512], P('ex'), may hold values from -0.0546875 to 0.0546875
- lengths: int32 [64], P('ex'), may hold values from 1 to 1024, as said below
- destination: int32 [64], P('ex'), may hold values from 0 to 63, each once
Outputs:
- scores: float32 [64, 16], P('ex', 'lay')
The draws below stay inside these ranges and needn't reach their ends.
Inputs may be any that keep to these rules, and one draw needn't show every extreme that they name: The lengths of one index of ex are its 2 packed examples in order; their sum is at most 2048, and in every draw some index of ex is exactly full. `destination`: each output row is named by exactly one packed example.
All inputs are finite; a program needn't handle non-finite values.
Results may differ from the reference program's by a relative error of at most 0.0042.
Values may be sent and summed in bfloat16 or wider, within the bound.
A program may use at most 128 MiB of HBM per device.

```python
import math
import jax
import jax.numpy as jnp
from jax import lax

DA = 5120
DG = 13824
QUERIES = 16
RANK = 32
EX_DEV = 2
TOK_DEV = 2048
LMAX = 1024
EXAMPLES = 64
TOKENS = 65536
N_EX = 32


def draw_lengths(key, part):
    key = jax.random.fold_in(key, 7)
    first_key, second_key = jax.random.split(key)
    blocks = EXAMPLES // EX_DEV
    drawn = jax.random.randint(first_key, (blocks, EX_DEV), 1, LMAX + 1)
    full_block = jax.random.randint(second_key, (), 0, blocks)
    rows = jnp.arange(blocks)[:, None]
    chosen = jnp.where(rows == full_block, LMAX, drawn)
    return chosen.reshape(-1).astype(jnp.int32)


def steps_of(key, extent, shards, low, largest):
    def one(axis_at, shards_of):
        draws = jax.random.uniform(jax.random.fold_in(jax.random.fold_in(key, 6), axis_at), (shards_of,), jnp.float32, low / len(shards), largest / len(shards))
        return jnp.repeat(jnp.exp(draws), extent[axis_at] // shards_of).reshape((-1,) + (1,) * (len(extent) - axis_at - 1))

    level = one(*shards[0])
    for cut in shards[1:]:
        level = level * one(*cut)
    return level


def noise(stream_key, shape, spread, most, shards=(), held_as=jnp.bfloat16):
    array = spread * jax.random.normal(stream_key, shape, jnp.float32)
    if shards:
        array = array * steps_of(stream_key, shape, shards, -0.22, 0.18)
    return jnp.clip(array, -most, most).astype(held_as)


def setup_inputs(seed: int = 0) -> dict:
    splits = jax.random.split(jax.random.key(seed), 9)
    return {
        "acts": noise(splits[0], (TOKENS, DA), 1.0, 6.0, ((0, 32), (1, 8))),
        "grads": noise(splits[1], (TOKENS, DG), 1.0, 6.0, ((0, 32), (1, 8))),
        "act_basis": noise(splits[2], (DA, DA), DA ** -0.5, 0.078125, ((0, 8), (1, 32))),
        "grad_basis": noise(splits[3], (DG, DG), DG ** -0.5, 0.0546875, ((0, 8), (1, 32))),
        "act_query": noise(splits[4], (DA, QUERIES * RANK), DA ** -0.5, 0.078125, ((0, 32),)),
        "grad_query": noise(splits[5], (DG, QUERIES * RANK), DG ** -0.5, 0.0546875, ((0, 32),)),
        "lengths": draw_lengths(jax.random.fold_in(splits[8], 71), 0),
        "destination": jax.random.permutation(splits[7], EXAMPLES).astype(jnp.int32),
    }


def reference(acts, grads, act_basis, grad_basis, act_query, grad_query, lengths, destination):
    grad_rot = jnp.dot(grad_basis, grad_query, preferred_element_type=jnp.float32).astype(jnp.bfloat16)
    act_rot = jnp.dot(act_basis, act_query, preferred_element_type=jnp.float32).astype(jnp.bfloat16)
    factor = 1.0 / math.sqrt(LMAX * RANK)

    def per_block(block):
        grad_rows, act_rows, block_lengths = block
        grad_proj = jnp.dot(grad_rows, grad_rot, preferred_element_type=jnp.float32)
        act_proj = jnp.dot(act_rows, act_rot, preferred_element_type=jnp.float32)
        token_score = lax.optimization_barrier(jnp.sum((grad_proj * act_proj).reshape(TOK_DEV, QUERIES, RANK), axis=2))
        ends = jnp.cumsum(block_lengths)
        starts = ends - block_lengths
        offsets = jnp.arange(TOK_DEV, dtype=jnp.int32)
        member = ((offsets[None, :] >= starts[:, None]) & (offsets[None, :] < ends[:, None])).astype(jnp.float32)
        return jnp.dot(member, token_score, precision=lax.Precision.HIGHEST) * factor
    packed = lax.map(per_block, (grads.reshape(N_EX, TOK_DEV, DG), acts.reshape(N_EX, TOK_DEV, DA), lengths.reshape(N_EX, EX_DEV)))
    packed = packed.reshape(EXAMPLES, QUERIES)
    return jnp.zeros((EXAMPLES, QUERIES), jnp.float32).at[destination].set(packed)
```

```python
import functools
import math

import jax
import jax.numpy as jnp
from jax import lax
from jax.experimental import pallas as pl
from jax.experimental.pallas import tpu as pltpu
from jax.sharding import PartitionSpec as P

RANK = 32
LMAX = 1024
NY, NZ, NX = 4, 8, 4
W = 128
MESH = pl.DeviceIdType.MESH
F32, BF16 = jnp.float32, jnp.bfloat16


class Plan:
    def __init__(self):
        self.tasks = []
        self.messages = 0

    def message(self, count=1):
        first = self.messages
        self.messages += count
        return first

    def task(self, emit, cost, after=(), arrivals=(), sends=(), rank=0):
        self.tasks.append((emit, cost, tuple(after), tuple(arrivals), tuple(sends), rank))
        return len(self.tasks) - 1

    def order(self):
        now, done, arrived, link_free, left, out = 0.0, {}, {}, {}, list(range(len(self.tasks))), []
        while left:
            best = None
            for at in left:
                _, cost, after, arrivals, _, rank = self.tasks[at]
                if any(a not in done for a in after) or any(m not in arrived for m in arrivals):
                    continue
                start = max([now] + [arrived[m] for m in arrivals])
                key = (start, rank, at)
                if best is None or key < best:
                    best = key
            start, _, at = best
            _, cost, _, _, sends, _ = self.tasks[at]
            now = start + cost
            done[at] = now
            for number, link, size in sends:
                rate, latency = (0.3, 0.8) if link == "core" else (0.06, 1.8)
                begin = max(now, link_free.get(link, 0.0))
                link_free[link] = begin + size / rate * 1e-3
                arrived[number] = link_free[link] + latency
            left.remove(at)
            out.append(at)
        return out


def kernel(lens, dest, acts, grads, abasis, gbasis, aquery, gquery, out,
           xa, xg, ba, bg, qa, qg, part, fin, rsbig, rssmall, acc, pown, psend, precv, xr, tsum, laybuf, exbuf,
           ins, ss, rs):
    ex, lay = lax.axis_index("ex"), lax.axis_index("lay")
    y, z = lax.div(ex, NZ), lax.rem(ex, NZ)
    x, c = lax.div(lay, 2), lax.rem(lay, 2)
    nf, na = gbasis.shape[0], abasis.shape[0]
    chunks = part.shape[0]
    rows = part.shape[1]
    tok = acts.shape[0]
    half = tok // 2
    quarter = half // NX
    small = rows // (NY * NZ)

    def wrap(v, n):
        return lax.rem(v + n, n)

    def yz(dy, dz):
        return (wrap(y + dy, NY) * NZ + wrap(z + dz, NZ), lay)

    def across(dx, dc=0):
        return (ex, wrap(x + dx, NX) * 2 + wrap(c + dc, 2))

    def copy(number, src, dst, device):
        return pltpu.make_async_remote_copy(src, dst, ss.at[number], rs.at[number], device_id=device, device_id_type=MESH)

    loads = [(gquery, qg), (gbasis, bg), (aquery, qa), (abasis, ba), (grads, xg), (acts, xa)]
    local = [pltpu.make_async_copy(src, dst, ins.at[i]) for i, (src, dst) in enumerate(loads)]
    for one in local:
        one.start()

    barrier = pltpu.get_barrier_semaphore()
    partners = [yz(i // NZ, i % NZ) for i in range(1, NY * NZ)] + [across(i // 2, i % 2) for i in range(1, 2 * NX)]
    for device in partners:
        pl.semaphore_signal(barrier, inc=1, device_id=device, device_id_type=MESH)

    plan = Plan()
    sent = []

    def post(number, src, dst, device):
        one = copy(number, src, dst, device)
        one.start()
        sent.append(one)

    def rotate(pair):
        def emit():
            if pair == 0:
                for one in local[:4]:
                    one.wait()
            cols = pl.ds(pair * 2 * W, 2 * W)

            def block(basis, query, size, count, base):
                def body(i, _):
                    at = pl.multiple_of(i * size, 16)
                    r = jnp.dot(basis[pl.ds(at, size), :], query[:, cols], preferred_element_type=F32)
                    to = pl.ds(pl.multiple_of(base + i * size, 16), size)
                    part[2 * pair, to, :] = r[:, :W]
                    part[2 * pair + 1, to, :] = r[:, W:]
                    return 0

                lax.fori_loop(0, count, body, 0)

            block(bg, qg, nf // 6, 6, 0)
            block(ba, qa, na // 2, 2, nf)
            for j in (2 * pair, 2 * pair + 1):
                part[j, nf + na :, :] = jnp.zeros((rows - nf - na, W), F32)
            if pair == 0:
                pl.semaphore_wait(barrier, len(partners))

        return emit

    rotated = [plan.task(rotate(0), 3.0)]
    rotated.append(plan.task(rotate(1), 0.7, after=rotated, rank=0))

    def reach(axis, step):
        return yz(step, 0) if axis == "y" else yz(0, step)

    def rs_chain(j, axis, sign, hops, src, buf, size, after, rank):
        pos, n = (y, NY) if axis == "y" else (z, NZ)
        number = [plan.message() for _ in range(hops)]
        prev = after
        for s in range(hops):
            def emit(s=s):
                piece = src(wrap(pos + sign * (hops - s), n))
                if s:
                    copy(number[s - 1], piece, buf(s - 1), reach(axis, sign)).wait_recv()
                    buf(s - 1)[...] += piece[...]
                    piece = buf(s - 1)
                post(number[s], piece, buf(s), reach(axis, sign))

            at = plan.task(emit, 0.15 if s else 0.05, after=prev, arrivals=[number[s - 1]] if s else [],
                           sends=[(number[s], axis + str(sign), size * W * 4e-3)], rank=rank)
            prev = [at]
        return number[-1], buf(hops - 1)

    def ag_chain(j, axis, sign, hops, ref, size, after, rank):
        pos, n = (y, NY) if axis == "y" else (z, NZ)
        number = [plan.message() for _ in range(hops)]
        prev = after
        for s in range(hops):
            def emit(s=s):
                if s:
                    mine = ref(wrap(pos - sign * s, n))
                    copy(number[s - 1], mine, mine, reach(axis, sign)).wait_recv()
                piece = ref(wrap(pos - sign * s, n))
                post(number[s], piece, piece, reach(axis, sign))

            at = plan.task(emit, 0.05, after=prev, arrivals=[number[s - 1]] if s else [],
                           sends=[(number[s], axis + str(sign), size * W * 2e-3)], rank=rank)
            prev = [at]

        def last():
            mine = ref(wrap(pos - sign * hops, n))
            copy(number[-1], mine, mine, reach(axis, sign)).wait_recv()

        return prev, number[-1], last

    def slab(ref, at, size):
        return ref.at[pl.ds(pl.multiple_of(at, 16), size), :]

    ready = []
    for j in range(chunks):
        zfirst = j % 2 == 0
        flip = 1 if j % 4 < 2 else -1
        begin = [rotated[j // 2]]
        rank = j
        if zfirst:
            mid = small * NY
            ends = [
                rs_chain(j, "z", flip, NZ // 2, lambda d, j=j: slab(part.at[j], d * mid, mid),
                         lambda s, j=j: rsbig.at[j, s], mid, begin, rank),
                rs_chain(j, "z", -flip, NZ // 2 - 1, lambda d, j=j: slab(part.at[j], d * mid, mid),
                         lambda s, j=j: rsbig.at[j, NZ // 2 + s], mid, begin, rank),
            ]

            def middle(j=j, ends=ends):
                for number, buf in ends:
                    copy(number, buf, buf, yz(0, 1)).wait_recv()
                acc[j, : small * NY, :] = slab(part.at[j], z * small * NY, small * NY)[...] + ends[0][1][...] + ends[1][1][...]

            at = plan.task(middle, 0.2, after=begin, arrivals=[n for n, _ in ends], rank=rank)
            ends2 = [
                rs_chain(j, "y", flip, NY // 2, lambda d, j=j: slab(acc.at[j], d * small, small),
                         lambda s, j=j: rssmall.at[j, s], small, [at], rank),
                rs_chain(j, "y", -flip, NY // 2 - 1, lambda d, j=j: slab(acc.at[j], d * small, small),
                         lambda s, j=j: rssmall.at[j, NY // 2 + s], small, [at], rank),
            ]

            def finish(j=j, ends2=ends2):
                for number, buf in ends2:
                    copy(number, buf, buf, yz(1, 0)).wait_recv()
                total = slab(acc.at[j], y * small, small)[...] + ends2[0][1][...] + ends2[1][1][...]
                slab(fin.at[j], z * small * NY + y * small, small)[...] = total.astype(BF16)

            at = plan.task(finish, 0.1, after=[at], arrivals=[n for n, _ in ends2], rank=rank)
            inner = [ag_chain(j, "y", s, h, lambda d, j=j: slab(fin.at[j], z * small * NY + d * small, small), small, [at], rank)
                     for s, h in ((flip, NY // 2), (-flip, NY // 2 - 1))]
            outer_of = [("z", flip, NZ // 2, lambda d, j=j: slab(fin.at[j], d * small * NY, small * NY), small * NY),
                        ("z", -flip, NZ // 2 - 1, lambda d, j=j: slab(fin.at[j], d * small * NY, small * NY), small * NY)]
        else:
            wide = small * NZ
            part_rows = wide // 2
            ends = []
            for k, sgn in ((0, flip), (1, -flip)):
                src = lambda d, j=j, k=k: slab(part.at[j], d * wide + k * part_rows, part_rows)
                ends.append(rs_chain(j, "y", sgn, NY // 2, src, lambda s, j=j, k=k: rsbig.at[j, 3 * k + s], part_rows, begin, rank))
                ends.append(rs_chain(j, "y", -sgn, NY // 2 - 1, src, lambda s, j=j, k=k: rsbig.at[j, 3 * k + 2 + s], part_rows, begin, rank))

            def middle(j=j, ends=ends, wide=wide, part_rows=part_rows):
                for number, buf in ends:
                    copy(number, buf, buf, yz(1, 0)).wait_recv()
                for k in (0, 1):
                    acc[j, k * part_rows : (k + 1) * part_rows, :] = (
                        slab(part.at[j], y * wide + k * part_rows, part_rows)[...] + ends[2 * k][1][...] + ends[2 * k + 1][1][...])

            at = plan.task(middle, 0.3, after=begin, arrivals=[n for n, _ in ends], rank=rank)
            ends2 = [
                rs_chain(j, "z", flip, NZ // 2, lambda d, j=j: slab(acc.at[j], d * small, small),
                         lambda s, j=j: rssmall.at[j, s], small, [at], rank),
                rs_chain(j, "z", -flip, NZ // 2 - 1, lambda d, j=j: slab(acc.at[j], d * small, small),
                         lambda s, j=j: rssmall.at[j, NZ // 2 + s], small, [at], rank),
            ]

            def finish(j=j, ends2=ends2, wide=wide):
                for number, buf in ends2:
                    copy(number, buf, buf, yz(0, 1)).wait_recv()
                total = slab(acc.at[j], z * small, small)[...] + ends2[0][1][...] + ends2[1][1][...]
                slab(fin.at[j], y * wide + z * small, small)[...] = total.astype(BF16)

            at = plan.task(finish, 0.1, after=[at], arrivals=[n for n, _ in ends2], rank=rank)
            inner = [ag_chain(j, "z", s, h, lambda d, j=j, wide=wide: slab(fin.at[j], y * wide + d * small, small), small, [at], rank)
                     for s, h in ((flip, NZ // 2), (-flip, NZ // 2 - 1))]
            outer_of = []
            for k, sgn in ((0, flip), (1, -flip)):
                ref = lambda d, j=j, k=k, wide=wide, part_rows=part_rows: slab(fin.at[j], d * wide + k * part_rows, part_rows)
                outer_of.append(("y", sgn, NY // 2, ref, part_rows))
                outer_of.append(("y", -sgn, NY // 2 - 1, ref, part_rows))

        def joined(inner=inner):
            for _, _, last in inner:
                last()

        at = plan.task(joined, 0.02, after=[a for prev, _, _ in inner for a in prev], arrivals=[n for _, n, _ in inner], rank=rank)
        outer = [ag_chain(j, a, s, h, ref, size, [at], rank) for a, s, h, ref, size in outer_of]

        def complete(outer=outer, j=j):
            for _, _, last in outer:
                last()
            if j == 0:
                for one in local[4:]:
                    one.wait()

        ready.append(plan.task(complete, 0.02, after=[a for prev, _, _ in outer for a in prev], arrivals=[n for _, n, _ in outer], rank=rank))

    size4 = quarter * W * 4e-3
    scored = []
    for j in range(chunks):
        rank = 10 + j
        to_core = plan.message(NX)

        def project(rows_at, store, j=j):
            token = pl.ds(pl.multiple_of(rows_at, 16), quarter)
            store(jnp.dot(xg[token, :], fin[j, :nf, :], preferred_element_type=F32),
                  jnp.dot(xa[token, :], fin[j, nf : nf + na, :], preferred_element_type=F32))

        def theirs(j=j, to_core=to_core, project=project):
            def body(i, _):
                q = lax.rem(x + 2 + i, NX)

                def store(g, a):
                    psend[j, i, 0] = g
                    psend[j, i, 1] = a

                project((1 - c) * half + q * quarter, store)
                copy(to_core + i, psend.at[j, i], precv.at[j, i], across(0, 1)).start()
                return 0

            lax.fori_loop(0, NX, body, 0)
            for i in range(NX):
                sent.append(copy(to_core + i, psend.at[j, i], precv.at[j, i], across(0, 1)))

        def ours(j=j, project=project):
            def body(i, _):
                q = lax.rem(x + 2 + i, NX)

                def store(g, a):
                    pown[j, i, 0] = g
                    pown[j, i, 1] = a

                project(c * half + q * quarter, store)
                return 0

            lax.fori_loop(0, NX, body, 0)

        at = plan.task(theirs, 1.3, after=[ready[j]], sends=[(to_core + i, "core", 2 * size4) for i in range(NX)], rank=rank)
        at = plan.task(ours, 1.3, after=[at], rank=rank)
        m = [plan.message() for _ in range(6)]

        def pair_sum(i, j=j, to_core=to_core):
            copy(to_core + i, psend.at[j, i], precv.at[j, i], across(0, 1)).wait_recv()
            pown[j, i] += precv[j, i]

        def far(j=j, m=m, pair_sum=pair_sum):
            pair_sum(0)
            post(m[0], pown.at[j, 0, 0], xr.at[j, 0], across(1))
            post(m[1], pown.at[j, 0, 1], xr.at[j, 1], across(-1))

        def near(j=j, m=m, pair_sum=pair_sum):
            pair_sum(1)
            pair_sum(3)
            post(m[2], pown.at[j, 1, 0], xr.at[j, 2], across(-1))
            post(m[3], pown.at[j, 3, 1], xr.at[j, 3], across(1))

        def relay(j=j, m=m):
            copy(m[0], xr.at[j, 0], xr.at[j, 0], across(1)).wait_recv()
            pown[j, 3, 0] += xr[j, 0]
            post(m[4], pown.at[j, 3, 0], xr.at[j, 4], across(1))
            copy(m[1], xr.at[j, 1], xr.at[j, 1], across(-1)).wait_recv()
            pown[j, 1, 1] += xr[j, 1]
            post(m[5], pown.at[j, 1, 1], xr.at[j, 5], across(-1))

        def score(j=j, m=m, pair_sum=pair_sum):
            pair_sum(2)
            for k in (2, 3, 4, 5):
                copy(m[k], xr.at[j, k], xr.at[j, k], across(1)).wait_recv()
            g = pown[j, 2, 0] + xr[j, 2] + xr[j, 4]
            a = pown[j, 2, 1] + xr[j, 3] + xr[j, 5]
            product = g * a
            token = c * half + x * quarter + lax.broadcasted_iota(jnp.int32, (quarter, W), 0)
            first, both = lens[0], lens[0] + lens[1]
            s0 = jnp.sum(jnp.where(token < first, product, 0.0), axis=0, keepdims=True)
            s1 = jnp.sum(jnp.where((token >= first) & (token < both), product, 0.0), axis=0, keepdims=True)
            row = lax.broadcasted_iota(jnp.int32, (8, W), 0)
            tsum[:, j * W : (j + 1) * W] = jnp.where(row == 0, s0, jnp.where(row == 1, s1, 0.0))

        a1 = plan.task(far, 0.2, after=[at], arrivals=[to_core], sends=[(m[0], "x1", size4), (m[1], "x-1", size4)], rank=rank)
        a2 = plan.task(near, 0.3, after=[a1], arrivals=[to_core + 1, to_core + 3],
                       sends=[(m[2], "x-1", size4), (m[3], "x1", size4)], rank=rank)
        a3 = plan.task(relay, 0.2, after=[a2], arrivals=[m[0], m[1]], sends=[(m[4], "x1", size4), (m[5], "x-1", size4)], rank=rank)
        scored.append(plan.task(score, 0.3, after=[a3], arrivals=[m[2], m[3], m[4], m[5], to_core + 2], rank=rank))

    for at in plan.order():
        plan.tasks[at][0]()

    used = plan.messages
    columns = chunks * W
    group = lax.broadcasted_iota(jnp.int32, (columns, W), 0) // RANK
    pick = (group == lax.broadcasted_iota(jnp.int32, (columns, W), 1)).astype(F32)
    laybuf[0] = jnp.dot(tsum[...], pick, precision=lax.Precision.HIGHEST, preferred_element_type=F32)
    for i in range(1, 2 * NX):
        post(used + i, laybuf.at[0], laybuf.at[i], across(i // 2, i % 2))
    total = laybuf[0]
    for i in range(1, 2 * NX):
        copy(used + i, laybuf.at[i], laybuf.at[i], across(i // 2, i % 2)).wait_recv()
        total = total + laybuf[i]
    used += 2 * NX
    factor = 1.0 / math.sqrt(LMAX * RANK)
    row = lax.broadcasted_iota(jnp.int32, (8, W), 0)
    lane = lax.broadcasted_iota(jnp.int32, (8, W), 1)
    named = jnp.where(row == 0, dest[0], jnp.where(row == 1, dest[1], -1)).astype(F32)
    exbuf[0] = jnp.where(lane == 16, named, total * factor)
    for i in range(1, NY * NZ):
        post(used + i, exbuf.at[0], exbuf.at[i], yz(i // NZ, i % NZ))
    for i in range(1, NY * NZ):
        copy(used + i, exbuf.at[i], exbuf.at[i], yz(i // NZ, i % NZ)).wait_recv()
    every = exbuf[...].reshape(NY * NZ * 8, W)
    target = every[:, 16:17]
    picked = []
    for r in range(2):
        hit = target == (2 * ex + r).astype(F32)
        one = jnp.sum(jnp.where(hit, every, 0.0), axis=0, keepdims=True)
        for k in range(2):
            at = lax.broadcasted_iota(jnp.int32, (1, W), 1) == 2 * lay + k
            picked.append(jnp.sum(jnp.where(at, one, 0.0), axis=1, keepdims=True))
    row = lax.broadcasted_iota(jnp.int32, (2, 2), 0)
    lane = lax.broadcasted_iota(jnp.int32, (2, 2), 1)
    out[...] = jnp.where(row == 0, jnp.where(lane == 0, picked[0], picked[1]), jnp.where(lane == 0, picked[2], picked[3]))

    for one in sent:
        one.wait_send()


def shards(acts, grads, act_basis, grad_basis, act_query, grad_query, lengths, destination):
    tok, na = acts.shape
    nf = grads.shape[1]
    columns = grad_query.shape[1]
    chunks = columns // W
    rows = -(-(nf + na) // (16 * NY * NZ)) * 16 * NY * NZ
    small = rows // (NY * NZ)
    quarter = tok // 8
    any_ = pl.BlockSpec(memory_space=pl.ANY)
    smem = pl.BlockSpec(memory_space=pltpu.SMEM)
    messages = 512
    return pl.pallas_call(
        kernel,
        out_shape=jax.ShapeDtypeStruct((2, 2), F32),
        in_specs=[smem, smem] + [any_] * 6,
        out_specs=pl.BlockSpec(memory_space=pltpu.VMEM),
        scratch_shapes=[
            pltpu.VMEM(acts.shape, BF16),
            pltpu.VMEM(grads.shape, BF16),
            pltpu.VMEM(act_basis.shape, BF16),
            pltpu.VMEM(grad_basis.shape, BF16),
            pltpu.VMEM(act_query.shape, BF16),
            pltpu.VMEM(grad_query.shape, BF16),
            pltpu.VMEM((chunks, rows, W), F32),
            pltpu.VMEM((chunks, rows, W), BF16),
            pltpu.VMEM((chunks, 7, small * NY, W), F32),
            pltpu.VMEM((chunks, 7, small, W), F32),
            pltpu.VMEM((chunks, small * NZ, W), F32),
            pltpu.VMEM((chunks, NX, 2, quarter, W), F32),
            pltpu.VMEM((chunks, NX, 2, quarter, W), F32),
            pltpu.VMEM((chunks, NX, 2, quarter, W), F32),
            pltpu.VMEM((chunks, 6, quarter, W), F32),
            pltpu.VMEM((8, columns), F32),
            pltpu.VMEM((2 * NX, 8, W), F32),
            pltpu.VMEM((NY * NZ, 8, W), F32),
            pltpu.SemaphoreType.DMA((6,)),
            pltpu.SemaphoreType.DMA((messages,)),
            pltpu.SemaphoreType.DMA((messages,)),
        ],
        compiler_params=pltpu.CompilerParams(collective_id=0, has_side_effects=True, vmem_limit_bytes=60 << 20),
        name="influence",
    )(lengths, destination, acts, grads, act_basis, grad_basis, act_query, grad_query)


def solution(mesh):
    return jax.shard_map(
        shards,
        mesh=mesh,
        in_specs=(
            P("ex", "lay"),
            P("ex", "lay"),
            P("lay", "ex"),
            P("lay", "ex"),
            P("ex", None),
            P("ex", None),
            P("ex"),
            P("ex"),
        ),
        out_specs=P("ex", "lay"),
        check_vma=False,
    )
```

```python
import functools
import math

import jax
import jax.numpy as jnp
from jax import lax
from jax.experimental import pallas as pl
from jax.experimental.pallas import tpu as pltpu
from jax.sharding import PartitionSpec as P

RANK = 32
LMAX = 1024
NY, NZ, NX = 4, 8, 4
W = 128
MESH = pl.DeviceIdType.MESH
F32, BF16 = jnp.float32, jnp.bfloat16


class Plan:
    def __init__(self):
        self.tasks = []
        self.messages = 0

    def message(self, count=1):
        first = self.messages
        self.messages += count
        return first

    def task(self, emit, cost, after=(), arrivals=(), sends=(), rank=0):
        self.tasks.append((emit, cost, tuple(after), tuple(arrivals), tuple(sends), rank))
        return len(self.tasks) - 1

    def order(self):
        now, done, arrived, link_free, left, out = 0.0, {}, {}, {}, list(range(len(self.tasks))), []
        while left:
            best = None
            for at in left:
                _, cost, after, arrivals, _, rank = self.tasks[at]
                if any(a not in done for a in after) or any(m not in arrived for m in arrivals):
                    continue
                start = max([now] + [arrived[m] for m in arrivals])
                key = (start, rank, at)
                if best is None or key < best:
                    best = key
            start, _, at = best
            _, cost, _, _, sends, _ = self.tasks[at]
            now = start + cost
            done[at] = now
            for number, link, size in sends:
                rate, latency = (0.3, 1.0) if link == "core" else (0.065, 4.0 if link == "zz" else 2.0)
                begin = max(now, link_free.get(link, 0.0))
                link_free[link] = begin + size / rate * 1e-3
                arrived[number] = link_free[link] + latency
            left.remove(at)
            out.append(at)
        return out


I16 = jnp.int16
TOP = 32000.0


def encode(value, scale):
    return jnp.floor(value * scale + 0.5).astype(jnp.int32).astype(I16)


def decode(code, unit):
    return code.astype(jnp.int32).astype(F32) * unit


def kernel(lens, dest, acts, grads, abasis, gbasis, aquery, gquery, out,
           xa, xg, ba, bg, qa, qg, qat, qgt, part, fin, ysend, ybuf, acc, zsend, zbuf, hy, hz, pown, psend, precv,
           xs, xr, tok, laybuf, exbuf, ins, ss, rs):
    ex, lay = lax.axis_index("ex"), lax.axis_index("lay")
    y, z = lax.div(ex, NZ), lax.rem(ex, NZ)
    x, c = lax.div(lay, 2), lax.rem(lay, 2)
    nf, na = gbasis.shape[1], abasis.shape[1]
    base = -(-nf // 128) * 128
    chunks, _, lanes = part.shape
    count = acts.shape[0]
    half = count // 2
    quarter = half // NX
    wide = lanes // NY
    short = W // NZ
    rows = W // 2

    def wrap(v, n):
        return lax.rem(v + n, n)

    def yz(dy, dz):
        return (wrap(y + dy, NY) * NZ + wrap(z + dz, NZ), lay)

    def across(dx, dc=0):
        return (ex, wrap(x + dx, NX) * 2 + wrap(c + dc, 2))

    def copy(number, src, dst, device):
        return pltpu.make_async_remote_copy(src, dst, ss.at[number], rs.at[number], device_id=device, device_id_type=MESH)

    loads = [(gquery, qg), (gbasis, bg), (aquery, qa), (abasis, ba), (grads, xg), (acts, xa)]
    local = [pltpu.make_async_copy(src, dst, ins.at[i]) for i, (src, dst) in enumerate(loads)]

    barrier = pltpu.get_barrier_semaphore()
    partners = [yz(0, 1), yz(0, -1), yz(1, 0), yz(-1, 0), across(1), across(-1), across(0, 1)]
    partners += [yz(2, 0)] + [yz(0, i) for i in range(2, NZ - 1)]
    for device in partners:
        pl.semaphore_signal(barrier, inc=1, device_id=device, device_id_type=MESH)
    for one in local:
        one.start()

    plan = Plan()
    sent = []

    def post(number, src, dst, device):
        one = copy(number, src, dst, device)
        one.start()
        sent.append(one)

    def fan(number, sends, whole):
        for src, dst, device in sends:
            copy(number, src, dst, device).start()
        sent.append(copy(number, whole, whole, yz(0, 1)))

    def landed(number, whole):
        copy(number, whole, whole, yz(0, 1)).wait_recv()

    def block(ref, row, height, lane, size):
        return ref.at[pl.ds(pl.multiple_of(row, 16), height), pl.ds(pl.multiple_of(lane, 128), size)]

    def piece(j, h, d):
        return block(part.at[j], h * rows, rows, d * wide, wide)

    def bounds(tile):
        return tile[0:1, 0:1], tile[0:1, 64:65]

    def spread(pair, d):
        lane = d * wide + lax.broadcasted_iota(jnp.int32, (1, wide), 1)
        return jnp.where(lane < base, pair[0], pair[1])

    hny, hnz = plan.message(), plan.message()
    state = {}

    def rot():
        local[0].wait()
        qgt[...] = qg[...].astype(F32).T.astype(BF16)
        local[2].wait()
        qat[...] = qa[...].astype(F32).T.astype(BF16)
        local[1].wait()
        largest = []
        for basis, query, size, at in ((bg, qgt, nf, 0), (ba, qat, na, base)):
            if size == na:
                local[3].wait()
            peak = jnp.zeros((1, 256), F32)
            for lo in range(0, size, 256):
                hi = min(lo + 256, size)
                r = jnp.dot(query[...], basis[:, lo:hi], preferred_element_type=F32)
                for j in range(chunks):
                    part[j, :, at + lo : at + hi] = r[j * W : (j + 1) * W]
                here = jnp.max(jnp.abs(r), axis=0, keepdims=True)
                if hi - lo < 256:
                    largest.append(jnp.max(here, axis=1, keepdims=True))
                else:
                    peak = jnp.maximum(peak, here)
            largest.append(jnp.max(peak, axis=1, keepdims=True))
        top_g, top_a = jnp.maximum(largest[0], largest[1]), jnp.maximum(largest[2], largest[3])
        for j in range(chunks):
            part[j, :, nf:base] = jnp.zeros((W, base - nf), F32)
            part[j, :, base + na :] = jnp.zeros((W, lanes - base - na), F32)
        lane = lax.broadcasted_iota(jnp.int32, (8, 128), 1)
        hy[0] = jnp.where(lane < 64, top_g, top_a)
        pl.semaphore_wait(barrier, len(partners))
        fan(hny, [(hy.at[0], hy.at[i], yz(i, 0)) for i in range(1, NY)], hy.at[1:NY])

    def scale_y():
        landed(hny, hy.at[1:NY])
        hz[0] = jnp.maximum(hy[0] + hy[1] + hy[2] + hy[3], 1e-30)
        fan(hnz, [(hz.at[0], hz.at[i], yz(0, i)) for i in range(1, NZ)], hz.at[1:NZ])
        state["unit"] = [b * (1.0 / TOP) for b in bounds(hz[0])]
        state["scale"] = [TOP / b for b in bounds(hz[0])]

    def scale_z():
        landed(hnz, hz.at[1:NZ])
        for i in range(1, NZ):
            state["unit", i] = [b * (1.0 / TOP) for b in bounds(hz[i])]

    begin = plan.task(rot, 4.0, sends=[(hny, "y0", 0.0)])
    begin = plan.task(scale_y, 0.5, after=[begin], arrivals=[hny], sends=[(hnz, "zz", 0.0)])
    begin2 = plan.task(scale_z, 0.5, after=[begin], arrivals=[hnz])

    ready = []
    for j in range(chunks):
        rank = j
        size = rows * wide * 2e-3
        signs = (1, -1)
        n = [[plan.message() for _ in range(3)] for _ in signs]

        def rs0(j=j, n=n):
            for h, sg in enumerate(signs):
                d = wrap(y + 2 * sg, NY)
                ysend[j, h, 0] = encode(piece(j, h, d)[...], spread(state["scale"], d))
                post(n[h][0], ysend.at[j, h, 0], ybuf.at[j, h, 0], yz(sg, 0))

        def rs1(j=j, n=n):
            for h, sg in enumerate(signs):
                d = wrap(y - sg, NY)
                ysend[j, h, 2] = encode(piece(j, h, d)[...], spread(state["scale"], d))
                post(n[h][2], ysend.at[j, h, 2], ybuf.at[j, h, 2], yz(-sg, 0))

        def rs2(h, sg, j=j, n=n):
            d = wrap(y + sg, NY)
            landed(n[h][0], ybuf.at[j, h, 0])
            total = piece(j, h, d)[...] + decode(ybuf[j, h, 0], spread(state["unit"], d))
            ysend[j, h, 1] = encode(total, spread(state["scale"], d))
            post(n[h][1], ysend.at[j, h, 1], ybuf.at[j, h, 1], yz(sg, 0))

        zn, zn2 = plan.message(), plan.message()

        def make_middle(zn=zn, j=j, n=n):
            def middle():
                unit, scale = spread(state["unit"], y), spread(state["scale"], y)
                for h in (0, 1):
                    landed(n[h][1], ybuf.at[j, h, 1])
                    landed(n[h][2], ybuf.at[j, h, 2])
                    total = piece(j, h, y)[...] + decode(ybuf[j, h, 1], unit) + decode(ybuf[j, h, 2], unit)
                    acc[j, h * rows : (h + 1) * rows, :] = total
                    zsend[j, h * rows : (h + 1) * rows, :] = encode(total, scale)
                fan(zn, [(block(zsend.at[j], wrap(z + i, NZ) * short, short, 0, wide), zbuf.at[j, i], yz(0, i))
                         for i in range(1, NZ)], zbuf.at[j, 1:NZ])

            return middle

        def finish(zn=zn, zn2=zn2, j=j):
            landed(zn, zbuf.at[j, 1:NZ])
            total = block(acc.at[j], z * short, short, 0, wide)[...]
            for i in range(1, NZ):
                total = total + decode(zbuf[j, i], spread(state["unit", i], y))
            mine = block(fin.at[j], z * short, short, y * wide, wide)
            mine[...] = total.astype(BF16)
            fan(zn2, [(mine, mine, yz(0, i)) for i in range(1, NZ)], zbuf.at[j, 1:NZ])

        a = [plan.message() for _ in range(6)]

        def fin_half(j, h, d):
            return block(fin.at[j], h * rows, rows, d * wide, wide)

        def ag0(zn2=zn2, a=a, j=j):
            landed(zn2, zbuf.at[j, 1:NZ])
            for h, sg in enumerate(signs):
                mine = fin_half(j, h, y)
                post(a[3 * h], mine, mine, yz(sg, 0))
            for h, sg in enumerate(signs):
                mine = fin_half(j, h, y)
                post(a[3 * h + 2], mine, mine, yz(-sg, 0))

        def ag1(h, sg, a=a, j=j):
            got = fin_half(j, h, wrap(y - sg, NY))
            landed(a[3 * h], got)
            post(a[3 * h + 1], got, got, yz(sg, 0))

        def complete(a=a, j=j):
            for h, sg in enumerate(signs):
                landed(a[3 * h + 1], fin_half(j, h, wrap(y - 2 * sg, NY)))
                landed(a[3 * h + 2], fin_half(j, h, wrap(y + sg, NY)))
            if j == 0:
                for one in local[4:]:
                    one.wait()

        t0 = plan.task(rs0, 0.3, after=[begin], sends=[(n[0][0], "y1", size), (n[1][0], "y-1", size)], rank=rank)
        t1 = plan.task(rs1, 0.3, after=[t0], sends=[(n[0][2], "y-1", size), (n[1][2], "y1", size)], rank=rank)
        t2 = []
        for h, sg in enumerate(signs):
            def rs2_of(h=h, sg=sg, rs2=rs2):
                rs2(h, sg)

            rs2_of.__name__ = "rs2"
            t2.append(plan.task(rs2_of, 0.3, after=[t0], arrivals=[n[h][0]], sends=[(n[h][1], "y%d" % sg, size)], rank=rank))
        t3 = plan.task(make_middle(), 1.0, after=t2 + [t1], arrivals=[n[0][1], n[0][2], n[1][1], n[1][2]],
                       sends=[(zn, "zz", 8 * short * wide * 2e-3)], rank=rank)
        t4 = plan.task(finish, 0.8, after=[t3, begin2], arrivals=[zn], sends=[(zn2, "zz", 8 * short * wide * 2e-3)], rank=rank)
        t5 = plan.task(ag0, 0.2, after=[t4], arrivals=[zn2], sends=[(a[0], "y1", size), (a[3], "y-1", size), (a[2], "y-1", size), (a[5], "y1", size)], rank=rank)
        t6 = []
        for h, sg in enumerate(signs):
            def ag1_of(h=h, sg=sg, ag1=ag1):
                ag1(h, sg)

            ag1_of.__name__ = "ag1"
            t6.append(plan.task(ag1_of, 0.1, after=[t5], arrivals=[a[3 * h]], sends=[(a[3 * h + 1], "y%d" % sg, size)], rank=rank))
        ready.append(plan.task(complete, 0.1, after=t6, arrivals=[a[1], a[2], a[4], a[5]], rank=rank))

    size4 = quarter * W * 4e-3
    size2 = quarter * (W + 16) * 2e-3
    tok[...] = jnp.zeros(tok.shape, F32)
    log2 = 1.0 / math.log(2.0)

    def pack(dst, value):
        bound = jnp.maximum(jnp.max(jnp.max(jnp.abs(value), axis=0, keepdims=True), axis=1, keepdims=True), 1e-30)
        power = jnp.ceil(jnp.log(bound) * log2)
        dst[:W, :] = encode(value, TOP * jnp.exp(power * (-1.0 / log2)))
        dst[W:, :] = jnp.broadcast_to(power, (16, quarter)).astype(jnp.int32).astype(I16)

    def unpack(src):
        power = src[W:, :].astype(jnp.int32).astype(F32)[0:1, 0:1]
        return decode(src[:W, :], jnp.exp(power * (1.0 / log2)) * (1.0 / TOP))

    for j in range(chunks):
        rank = 10 + j
        to_core = plan.message(NX)

        def project(at, store, j=j):
            token = pl.ds(pl.multiple_of(at, 128), quarter)
            store[0] = jnp.dot(fin[j, :, :nf], xg[:, token], preferred_element_type=F32)
            store[1] = lax.dot_general(fin[j, :, base : base + na], xa[token, :], (((1,), (1,)), ((), ())), preferred_element_type=F32)

        prev = [ready[j]]
        mine = []
        for i in range(NX):
            def theirs(i=i, j=j, to_core=to_core, project=project):
                project((1 - c) * half + lax.rem(x + 2 + i, NX) * quarter, psend.at[j, i])
                post(to_core + i, psend.at[j, i], precv.at[j, i], across(0, 1))

            prev = [plan.task(theirs, 0.5, after=prev, sends=[(to_core + i, "core", 2 * size4)], rank=rank)]
        for i in range(NX):
            def ours(i=i, j=j, project=project):
                project(c * half + lax.rem(x + 2 + i, NX) * quarter, pown.at[j, i])

            prev = [plan.task(ours, 0.5, after=prev, rank=rank)]
            mine.append(prev[0])
        m = [plan.message() for _ in range(6)]

        def pair_sum(i, j=j, to_core=to_core):
            landed(to_core + i, precv.at[j, i])
            pown[j, i] += precv[j, i]

        def send(k, value, dx, j=j, m=m):
            pack(xs.at[j, k], value)
            post(m[k], xs.at[j, k], xr.at[j, k], across(dx))

        def arrived(k, j=j, m=m):
            landed(m[k], xr.at[j, k])
            return unpack(xr.at[j, k])

        def far(j=j, send=send, pair_sum=pair_sum):
            pair_sum(0)
            send(0, pown[j, 0, 0], 1)
            send(1, pown[j, 0, 1], -1)

        def near(j=j, send=send, pair_sum=pair_sum):
            pair_sum(1)
            send(2, pown[j, 1, 0], -1)

        def near2(j=j, send=send, pair_sum=pair_sum):
            pair_sum(3)
            send(3, pown[j, 3, 1], 1)

        def relay(j=j, send=send, arrived=arrived):
            send(4, pown[j, 3, 0] + arrived(0), 1)
            send(5, pown[j, 1, 1] + arrived(1), -1)

        def score(j=j, arrived=arrived, pair_sum=pair_sum):
            pair_sum(2)
            g = pown[j, 2, 0] + arrived(2) + arrived(4)
            a = pown[j, 2, 1] + arrived(3) + arrived(5)
            tok[j * W // RANK : (j + 1) * W // RANK, :] = jnp.sum((g * a).reshape(W // RANK, RANK, quarter), axis=1)

        a1 = plan.task(far, 0.6, after=[mine[0]], arrivals=[to_core], sends=[(m[0], "x1", size2), (m[1], "x-1", size2)], rank=rank)
        a2 = plan.task(near, 0.4, after=[a1, mine[1]], arrivals=[to_core + 1], sends=[(m[2], "x-1", size2)], rank=rank)
        a2 = plan.task(near2, 0.4, after=[a2, mine[3]], arrivals=[to_core + 3], sends=[(m[3], "x1", size2)], rank=rank)
        a3 = plan.task(relay, 0.6, after=[a2], arrivals=[m[0], m[1]], sends=[(m[4], "x1", size2), (m[5], "x-1", size2)], rank=rank)
        plan.task(score, 0.6, after=[a3], arrivals=[m[2], m[3], m[4], m[5], to_core + 2], rank=rank)

    for at in plan.order():
        plan.tasks[at][0]()

    used = plan.messages
    row = lax.broadcasted_iota(jnp.int32, (8, quarter), 0)
    token = c * half + x * quarter + lax.broadcasted_iota(jnp.int32, (8, quarter), 1)
    lo = jnp.where(row == 0, 0, lens[0])
    hi = jnp.where(row == 0, lens[0], jnp.where(row == 1, lens[0] + lens[1], 0))
    member = ((token >= lo) & (token < hi)).astype(F32)
    laybuf[0] = lax.dot_general(member, tok[...], (((1,), (1,)), ((), ())), precision=lax.Precision.HIGHEST,
                                preferred_element_type=F32)
    fan(used, [(laybuf.at[0], laybuf.at[i], across(i // 2, i % 2)) for i in range(1, 2 * NX)], laybuf.at[1 : 2 * NX])
    landed(used, laybuf.at[1 : 2 * NX])
    total = laybuf[0]
    for i in range(1, 2 * NX):
        total = total + laybuf[i]
    factor = 1.0 / math.sqrt(LMAX * RANK)
    row = lax.broadcasted_iota(jnp.int32, (8, W), 0)
    lane = lax.broadcasted_iota(jnp.int32, (8, W), 1)
    named = jnp.where(row == 0, dest[0], jnp.where(row == 1, dest[1], -1)).astype(F32)
    exbuf[0] = jnp.where(lane == 16, named, total * factor)
    fan(used + 1, [(exbuf.at[0], exbuf.at[i], yz(i // NZ, i % NZ)) for i in range(1, NY * NZ)], exbuf.at[1 : NY * NZ])
    landed(used + 1, exbuf.at[1 : NY * NZ])
    every = exbuf[...].reshape(NY * NZ * 8, W)
    target = every[:, 16:17]
    picked = []
    for r in range(2):
        hit = target == (2 * ex + r).astype(F32)
        one = jnp.sum(jnp.where(hit, every, 0.0), axis=0, keepdims=True)
        for k in range(2):
            at = lax.broadcasted_iota(jnp.int32, (1, W), 1) == 2 * lay + k
            picked.append(jnp.sum(jnp.where(at, one, 0.0), axis=1, keepdims=True))
    row = lax.broadcasted_iota(jnp.int32, (2, 2), 0)
    lane = lax.broadcasted_iota(jnp.int32, (2, 2), 1)
    out[...] = jnp.where(row == 0, jnp.where(lane == 0, picked[0], picked[1]), jnp.where(lane == 0, picked[2], picked[3]))

    for one in sent:
        one.wait_send()


def shards(acts, grads, act_basis, grad_basis, act_query, grad_query, lengths, destination):
    grads, act_basis, grad_basis = grads.T, act_basis.T, grad_basis.T
    count, na = acts.shape
    nf = grads.shape[0]
    columns = grad_query.shape[1]
    chunks = columns // W
    tiles = -(-nf // 128) + -(-na // 128)
    lanes = -(-tiles // NY) * NY * 128
    short, wide = W // NZ, lanes // NY
    quarter = count // (2 * NX)
    any_ = pl.BlockSpec(memory_space=pl.ANY)
    smem = pl.BlockSpec(memory_space=pltpu.SMEM)
    messages = 2 + chunks * 24 + 2
    return pl.pallas_call(
        kernel,
        out_shape=jax.ShapeDtypeStruct((2, 2), F32),
        in_specs=[smem, smem] + [any_] * 6,
        out_specs=pl.BlockSpec(memory_space=pltpu.VMEM),
        scratch_shapes=[
            pltpu.VMEM(acts.shape, BF16),
            pltpu.VMEM(grads.shape, BF16),
            pltpu.VMEM(act_basis.shape, BF16),
            pltpu.VMEM(grad_basis.shape, BF16),
            pltpu.VMEM(act_query.shape, BF16),
            pltpu.VMEM(grad_query.shape, BF16),
            pltpu.VMEM(act_query.shape[::-1], BF16),
            pltpu.VMEM(grad_query.shape[::-1], BF16),
            pltpu.VMEM((chunks, W, lanes), F32),
            pltpu.VMEM((chunks, W, lanes), BF16),
            pltpu.VMEM((chunks, 2, 3, W // 2, wide), I16),
            pltpu.VMEM((chunks, 2, 3, W // 2, wide), I16),
            pltpu.VMEM((chunks, W, wide), F32),
            pltpu.VMEM((chunks, W, wide), I16),
            pltpu.VMEM((chunks, NZ, short, wide), I16),
            pltpu.VMEM((NY, 8, 128), F32),
            pltpu.VMEM((NZ, 8, 128), F32),
            pltpu.VMEM((chunks, NX, 2, W, quarter), F32),
            pltpu.VMEM((chunks, NX, 2, W, quarter), F32),
            pltpu.VMEM((chunks, NX, 2, W, quarter), F32),
            pltpu.VMEM((chunks, 6, W + 16, quarter), I16),
            pltpu.VMEM((chunks, 6, W + 16, quarter), I16),
            pltpu.VMEM((128, quarter), F32),
            pltpu.VMEM((2 * NX, 8, 128), F32),
            pltpu.VMEM((NY * NZ, 8, 128), F32),
            pltpu.SemaphoreType.DMA((6,)),
            pltpu.SemaphoreType.DMA((messages,)),
            pltpu.SemaphoreType.DMA((messages,)),
        ],
        compiler_params=pltpu.CompilerParams(collective_id=0, has_side_effects=True, vmem_limit_bytes=60 << 20),
        name="influence",
    )(lengths, destination, acts, grads, act_basis, grad_basis, act_query, grad_query)


def solution(mesh):
    return jax.shard_map(
        shards,
        mesh=mesh,
        in_specs=(
            P("ex", "lay"),
            P("ex", "lay"),
            P("lay", "ex"),
            P("lay", "ex"),
            P("ex", None),
            P("ex", None),
            P("ex"),
            P("ex"),
        ),
        out_specs=P("ex", "lay"),
        check_vma=False,
    )
```

```python
import functools
import math

import jax
import jax.numpy as jnp
from jax import lax
from jax.experimental import pallas as pl
from jax.experimental.pallas import tpu as pltpu
from jax.sharding import PartitionSpec as P

RANK = 32
LMAX = 1024
NY, NZ, NX = 4, 8, 4
W = 128
MESH = pl.DeviceIdType.MESH
F32, BF16 = jnp.float32, jnp.bfloat16


class Plan:
    def __init__(self):
        self.tasks = []
        self.messages = 0
        self.groups = 0

    def message(self, count=1):
        first = self.messages
        self.messages += count
        return first

    def group(self):
        self.groups += 1
        return self.groups - 1

    def task(self, emit, cost, after=(), arrivals=(), sends=(), rank=0):
        self.tasks.append((emit, cost, tuple(after), tuple(arrivals), tuple(sends), rank))
        return len(self.tasks) - 1

    def order(self):
        now, done, arrived, link_free, left, out = 0.0, {}, {}, {}, list(range(len(self.tasks))), []
        while left:
            best = None
            for at in left:
                _, cost, after, arrivals, _, rank = self.tasks[at]
                if any(a not in done for a in after) or any(m not in arrived for m in arrivals):
                    continue
                start = max([now] + [arrived[m] for m in arrivals])
                key = (start, rank, at)
                if best is None or key < best:
                    best = key
            start, _, at = best
            _, cost, _, _, sends, _ = self.tasks[at]
            now = start + cost
            done[at] = now
            for number, link, size in sends:
                rate, latency = (0.3, 2.5) if link == "core" else (0.062, 4.0 if link[0] == "x" else 2.2)
                begin = max(now, link_free.get(link, 0.0))
                link_free[link] = begin + size / rate * 1e-3
                arrived[number] = link_free[link] + latency
            left.remove(at)
            out.append(at)
        return out


I16 = jnp.int16
TOP = 32000.0


def encode(value, scale):
    return jnp.floor(value * scale + 0.5).astype(jnp.int32).astype(I16)


def decode(code, unit):
    return code.astype(jnp.int32).astype(F32) * unit


def kernel(lens, dest, acts, grads, abasis, gbasis, aquery, gquery, out,
           xa, xg, ba, bg, qa, qg, qat, qgt, part, fin, ysend, ybuf, acc, zsend, zbuf, relayed, hy, hz, pfull, precv,
           xs, xr, pairs, exbuf, ins, ss, rs):
    ex, lay = lax.axis_index("ex"), lax.axis_index("lay")
    y, z = lax.div(ex, NZ), lax.rem(ex, NZ)
    x, c = lax.div(lay, 2), lax.rem(lay, 2)
    nf, na = gbasis.shape[1], abasis.shape[1]
    base = -(-nf // 128) * 128
    chunks, _, lanes = part.shape
    count = acts.shape[0]
    tile = count // 8
    own = W // 2
    each = own // NX
    wide = lanes // NY
    short = W // NZ
    rows = W // 2

    def wrap(v, n):
        return lax.rem(v + n, n)

    def yz(dy, dz):
        return (wrap(y + dy, NY) * NZ + wrap(z + dz, NZ), lay)

    def across(dx, dc=0):
        return (ex, wrap(x + dx, NX) * 2 + wrap(c + dc, 2))

    def copy(number, src, dst, device, group=0):
        return pltpu.make_async_remote_copy(src, dst, ss.at[group], rs.at[number], device_id=device, device_id_type=MESH)

    loads = [(gquery, qg), (gbasis, bg), (aquery, qa), (abasis, ba), (grads, xg), (acts, xa)]
    local = [pltpu.make_async_copy(src, dst, ins.at[i]) for i, (src, dst) in enumerate(loads)]

    barrier = pltpu.get_barrier_semaphore()
    partners = [yz(0, 1), yz(0, -1), yz(1, 0), yz(-1, 0), across(1), across(-1), across(0, 1)]
    partners += [yz(2, 0)] + [yz(0, i) for i in range(2, NZ - 1)]
    for device in partners:
        pl.semaphore_signal(barrier, inc=1, device_id=device, device_id_type=MESH)
    for one in local:
        one.start()

    plan = Plan()
    sent = []

    def group(whole):
        number = plan.group()
        sent.append(copy(0, whole, whole, yz(0, 1), number))
        return number

    def post(number, src, dst, device, of):
        copy(number, src, dst, device, of).start()

    def fan(number, sends, of):
        for src, dst, device in sends:
            copy(number, src, dst, device, of).start()

    def landed(number, whole):
        copy(number, whole, whole, yz(0, 1)).wait_recv()

    def block(ref, row, height, lane, size):
        return ref.at[pl.ds(pl.multiple_of(row, 16), height), pl.ds(pl.multiple_of(lane, 128), size)]

    def piece(j, h, d):
        return block(part.at[j], h * rows, rows, d * wide, wide)

    def bounds(tile):
        return tile[0:1, 0:1], tile[0:1, 64:65]

    def spread(pair, d):
        lane = d * wide + lax.broadcasted_iota(jnp.int32, (1, wide), 1)
        return jnp.where(lane < base, pair[0], pair[1])

    def arrange(rows_of):
        out_rows = []
        for j in range(chunks):
            for core in range(2):
                for at in range(NX):
                    for q in (4 * at + 2 * core, 4 * at + 2 * core + 1):
                        out_rows.append(rows_of[q * RANK + 8 * j : q * RANK + 8 * j + 8])
        return jnp.concatenate(out_rows, axis=0).astype(BF16)

    hny, hnz = plan.message(), plan.message()
    state = {}

    def rot():
        local[0].wait()
        qgt[...] = arrange(qg[...].astype(F32).T)
        local[2].wait()
        qat[...] = arrange(qa[...].astype(F32).T)
        local[1].wait()
        largest = []
        for basis, query, size, at in ((bg, qgt, nf, 0), (ba, qat, na, base)):
            if size == na:
                local[3].wait()
            peak = jnp.zeros((1, 256), F32)
            for lo in range(0, size, 256):
                hi = min(lo + 256, size)
                r = jnp.dot(query[...], basis[:, lo:hi], preferred_element_type=F32)
                for j in range(chunks):
                    part[j, :, at + lo : at + hi] = r[j * W : (j + 1) * W]
                here = jnp.max(jnp.abs(r), axis=0, keepdims=True)
                if hi - lo < 256:
                    largest.append(jnp.max(here, axis=1, keepdims=True))
                else:
                    peak = jnp.maximum(peak, here)
            largest.append(jnp.max(peak, axis=1, keepdims=True))
        top_g, top_a = jnp.maximum(largest[0], largest[1]), jnp.maximum(largest[2], largest[3])
        for j in range(chunks):
            part[j, :, nf:base] = jnp.zeros((W, base - nf), F32)
            part[j, :, base + na :] = jnp.zeros((W, lanes - base - na), F32)
        lane = lax.broadcasted_iota(jnp.int32, (8, 128), 1)
        hy[0] = jnp.maximum(jnp.where(lane < 64, top_g, top_a), 1e-30)
        state["first"] = [TOP / b for b in bounds(hy[0])]
        pl.semaphore_wait(barrier, len(partners))
        fan(hny, [(hy.at[0], hy.at[i], yz(i, 0)) for i in range(1, NY)], group(hy.at[1:NY]))

    def scale_y():
        landed(hny, hy.at[1:NY])
        hz[0] = hy[0] + hy[1] + hy[2] + hy[3]
        for i in (1, 3):
            state["y", i] = [b * (1.0 / TOP) for b in bounds(hy[i])]
        fan(hnz, [(hz.at[0], hz.at[i], yz(0, i)) for i in range(1, NZ)], group(hz.at[1:NZ]))
        state["unit"] = [b * (1.0 / TOP) for b in bounds(hz[0])]
        state["scale"] = [TOP / b for b in bounds(hz[0])]

    def scale_z():
        landed(hnz, hz.at[1:NZ])
        for turn in (1, -1):
            for mine, over in ((0, turn), (0, -turn)):
                total = hz[0] + hz[over % NZ]
                state["two", over % NZ] = [TOP / b for b in bounds(total)]
            for k in (1, 3, -2):
                total = hz[turn * k % NZ] + hz[turn * (k + (1 if k > 0 else -1)) % NZ]
                state["sum", turn * k % NZ] = [b * (1.0 / TOP) for b in bounds(total)]
            state["z", turn % NZ] = [b * (1.0 / TOP) for b in bounds(hz[turn % NZ])]

    begin = plan.task(rot, 4.0, sends=[(hny, "y0", 0.0)])
    scaled = plan.task(scale_y, 0.3, after=[begin], arrivals=[hny], sends=[(hnz, "zz", 0.0)], rank=-1)
    begin2 = plan.task(scale_z, 0.3, after=[scaled], arrivals=[hnz], rank=-1)
    chain = {"t0": [begin], "t1": [], "t2": []}

    ready = []
    for j in range(chunks):
        rank = j
        size = rows * wide * 2e-3
        signs = (1, -1)
        n = [[plan.message() for _ in range(3)] for _ in signs]
        gy, gz, gz2, gy2 = group(ysend.at[j]), group(zbuf.at[j, 1:NZ]), group(zbuf.at[j, 1:NZ]), group(ysend.at[j])
        turn = 1 if j % 2 == 0 else -1

        def rs0(j=j, n=n, gy=gy):
            for h, sg in enumerate(signs):
                d = wrap(y + 2 * sg, NY)
                ysend[j, h, 0] = encode(piece(j, h, d)[...], spread(state["first"], d))
                post(n[h][0], ysend.at[j, h, 0], ybuf.at[j, h, 0], yz(sg, 0), gy)

        def rs1(j=j, n=n, gy=gy):
            for h, sg in enumerate(signs):
                d = wrap(y - sg, NY)
                ysend[j, h, 2] = encode(piece(j, h, d)[...], spread(state["first"], d))
                post(n[h][2], ysend.at[j, h, 2], ybuf.at[j, h, 2], yz(-sg, 0), gy)

        def rs2(h, sg, j=j, n=n, gy=gy):
            d = wrap(y + sg, NY)
            landed(n[h][0], ybuf.at[j, h, 0])
            total = piece(j, h, d)[...] + decode(ybuf[j, h, 0], spread(state["y", sg % NY], d))
            ysend[j, h, 1] = encode(total, spread(state["scale"], d))
            post(n[h][1], ysend.at[j, h, 1], ybuf.at[j, h, 1], yz(sg, 0), gy)

        zn = [plan.message() for _ in range(4)]

        def zrows(ref, step, j=j):
            return block(ref.at[j], wrap(z + step, NZ) * short, short, 0, wide)

        def middle(j=j, n=n, zn=zn, gz=gz, t=turn, zrows=zrows):
            unit, scale = spread(state["unit"], y), spread(state["scale"], y)
            other = [spread(state["y", -sg % NY], y) for sg in signs]
            for h in (0, 1):
                landed(n[h][1], ybuf.at[j, h, 1])
                landed(n[h][2], ybuf.at[j, h, 2])
                total = piece(j, h, y)[...] + decode(ybuf[j, h, 1], unit) + decode(ybuf[j, h, 2], other[h])
                acc[j, h * rows : (h + 1) * rows, :] = total
                zsend[j, h * rows : (h + 1) * rows, :] = encode(total, scale)
            fan(zn[0], [(zrows(zsend, 4), zbuf.at[j, 0], yz(0, t)), (zrows(zsend, 2 * t), zbuf.at[j, 1], yz(0, t)),
                        (zrows(zsend, -3 * t), zbuf.at[j, 2], yz(0, -t))], gz)
            fan(zn[1], [(zrows(zsend, -t), zbuf.at[j, 3], yz(0, -t))], gz)

        def relay_z(j=j, zn=zn, gz=gz, t=turn, zrows=zrows):
            landed(zn[0], zbuf.at[j, 0:3])
            near = spread(state["z", t % NZ], y)
            far = spread(state["z", -t % NZ], y)
            ahead, back = spread(state["two", t % NZ], y), spread(state["two", -t % NZ], y)
            for k, (got, step, unit, scale) in enumerate(((0, 3 * t, near, ahead), (1, t, near, ahead), (2, -2 * t, far, back))):
                relayed[j, k] = encode(zrows(acc, step)[...] + decode(zbuf[j, got], unit), scale)
            fan(zn[1], [(relayed.at[j, k], zbuf.at[j, 4 + k], yz(0, step)) for k, step in ((0, 3 * t), (1, t), (2, -2 * t))], gz)

        def finish(j=j, zn=zn, gz2=gz2, t=turn, zrows=zrows):
            landed(zn[1], zbuf.at[j, 3:7])
            total = zrows(acc, 0)[...] + decode(zbuf[j, 3], spread(state["z", -t % NZ], y))
            for k, step in ((4, 3 * t), (5, t), (6, -2 * t)):
                total = total + decode(zbuf[j, k], spread(state["sum", step % NZ], y))
            mine = block(fin.at[j], z * short, short, y * wide, wide)
            mine[...] = total.astype(BF16)
            fan(zn[2], [(mine, mine, yz(0, step)) for step in (3 * t, t, -t, -2 * t)], gz2)

        def spread_z(j=j, zn=zn, gz2=gz2, t=turn):
            landed(zn[2], zbuf.at[j, 0:4])
            for step, to in ((-3 * t, t), (-t, t), (2 * t, -t)):
                got = block(fin.at[j], wrap(z + step, NZ) * short, short, y * wide, wide)
                fan(zn[3], [(got, got, yz(0, to))], gz2)

        a = [plan.message() for _ in range(6)]

        def fin_half(j, h, d):
            return block(fin.at[j], h * rows, rows, d * wide, wide)

        def ag0(zn=zn, a=a, j=j, gy2=gy2):
            landed(zn[3], zbuf.at[j, 0:3])
            for h, sg in enumerate(signs):
                mine = fin_half(j, h, y)
                post(a[3 * h], mine, mine, yz(sg, 0), gy2)
            for h, sg in enumerate(signs):
                mine = fin_half(j, h, y)
                post(a[3 * h + 2], mine, mine, yz(-sg, 0), gy2)

        def ag1(h, sg, a=a, j=j, gy2=gy2):
            got = fin_half(j, h, wrap(y - sg, NY))
            landed(a[3 * h], got)
            post(a[3 * h + 1], got, got, yz(sg, 0), gy2)

        def complete(a=a, j=j):
            for h, sg in enumerate(signs):
                landed(a[3 * h + 1], fin_half(j, h, wrap(y - 2 * sg, NY)))
                landed(a[3 * h + 2], fin_half(j, h, wrap(y + sg, NY)))
            if j == 0:
                for one in local[4:]:
                    one.wait()

        t0 = plan.task(rs0, 0.3, after=chain["t0"], sends=[(n[0][0], "y1", size), (n[1][0], "y-1", size)], rank=rank)
        t1 = plan.task(rs1, 0.3, after=chain["t1"] + [t0], sends=[(n[0][2], "y-1", size), (n[1][2], "y1", size)], rank=rank)
        t2 = []
        for h, sg in enumerate(signs):
            def rs2_of(h=h, sg=sg, rs2=rs2):
                rs2(h, sg)

            rs2_of.__name__ = "rs2"
            t2.append(plan.task(rs2_of, 0.3, after=[t0, scaled], arrivals=[n[h][0]], sends=[(n[h][1], "y%d" % sg, size)], rank=rank))
        chain["t0"], chain["t1"] = [t1] if j == 0 else chain["t2"], t2
        chain["t2"] = t2
        unit_z = short * wide * 2e-3
        t3 = plan.task(middle, 0.6, after=t2 + [t1], arrivals=[n[0][1], n[0][2], n[1][1], n[1][2]],
                       sends=[(zn[0], "z%d" % turn, 2 * unit_z), (zn[1], "z%d" % -turn, 2 * unit_z)], rank=rank)
        t3 = plan.task(relay_z, 0.3, after=[t3, begin2], arrivals=[zn[0]],
                       sends=[(zn[1], "z%d" % turn, 4 * unit_z), (n[0][0], "z%d" % -turn, 2 * unit_z)], rank=rank)
        t4 = plan.task(finish, 0.3, after=[t3], arrivals=[zn[1]],
                       sends=[(zn[2], "z%d" % turn, 4 * unit_z), (n[0][0], "z%d" % -turn, 3 * unit_z)], rank=rank)
        t4 = plan.task(spread_z, 0.1, after=[t4], arrivals=[zn[2]],
                       sends=[(zn[3], "z%d" % turn, 2 * unit_z), (n[0][0], "z%d" % -turn, unit_z)], rank=rank)
        t5 = plan.task(ag0, 0.2, after=[t4], arrivals=[zn[3]], sends=[(a[0], "y1", size), (a[3], "y-1", size), (a[2], "y-1", size), (a[5], "y1", size)], rank=rank)
        t6 = []
        for h, sg in enumerate(signs):
            def ag1_of(h=h, sg=sg, ag1=ag1):
                ag1(h, sg)

            ag1_of.__name__ = "ag1"
            t6.append(plan.task(ag1_of, 0.1, after=[t5], arrivals=[a[3 * h]], sends=[(a[3 * h + 1], "y%d" % sg, size)], rank=rank))
        ready.append(plan.task(complete, 0.1, after=t6, arrivals=[a[1], a[2], a[4], a[5]], rank=rank))

    size4 = 4 * tile * own * 4e-3
    size2 = each * (count + 128) * 2e-3
    pairs[...] = jnp.zeros(pairs.shape, F32)
    log2 = 1.0 / math.log(2.0)

    def pack(dst, value):
        bound = jnp.maximum(jnp.max(jnp.max(jnp.abs(value), axis=0, keepdims=True), axis=1, keepdims=True), 1e-30)
        power = jnp.ceil(jnp.log(bound) * log2)
        dst[:, :count] = encode(value, TOP * jnp.exp(power * (-1.0 / log2)))
        dst[:, count:] = jnp.broadcast_to(power, (each, 128)).astype(jnp.int32).astype(I16)

    def unpack(src):
        power = src[:, count:].astype(jnp.int32).astype(F32)[0:1, 0:1]
        return decode(src[:, :count], jnp.exp(power * (1.0 / log2)) * (1.0 / TOP))

    for j in range(chunks):
        rank = 10 + j
        to_core = plan.message()
        gc, gx = group(precv.at[j]), group(xs.at[j])

        def theirs_block(j, i):
            return pfull.at[j, :, pl.ds(pl.multiple_of((1 - c) * own, 16), own), 2 * i * tile : 2 * (i + 1) * tile]

        def there_block(j, i):
            return precv.at[j, :, :, 2 * i * tile : 2 * (i + 1) * tile]

        prev = [ready[j]]
        for i in range(8):
            def project(i=i, j=j, gc=gc, to_core=to_core, theirs_block=theirs_block, there_block=there_block):
                token = slice(i * tile, (i + 1) * tile)
                pfull[j, 0, :, token] = jnp.dot(fin[j, :, :nf], xg[:, token], preferred_element_type=F32)
                pfull[j, 1, :, token] = lax.dot_general(
                    fin[j, :, base : base + na], xa[token, :], (((1,), (1,)), ((), ())), preferred_element_type=F32)
                if i % 2:
                    post(to_core, theirs_block(j, i // 2), there_block(j, i // 2), across(0, 1), gc)

            prev = [plan.task(project, 0.27, after=prev, sends=[(to_core, "core", size4)] if i % 2 else [], rank=rank)]
        m = [plan.message() for _ in range(6)]

        def pair(k, dx, j=j):
            to = wrap(x + dx, NX) * each
            return (pfull[j, k, pl.ds(pl.multiple_of(c * own + to, 16), each), :]
                    + precv[j, k, pl.ds(pl.multiple_of(to, 16), each), :])

        def send(k, value, dx, j=j, m=m, gx=gx):
            pack(xs.at[j, k], value)
            post(m[k], xs.at[j, k], xr.at[j, k], across(dx), gx)

        def arrived(k, j=j, m=m):
            landed(m[k], xr.at[j, k])
            return unpack(xr.at[j, k])

        def far(j=j, send=send, pair=pair, to_core=to_core):
            landed(to_core, precv.at[j])
            send(0, pair(0, 2), 1)
            send(1, pair(1, 2), -1)

        def near(send=send, pair=pair):
            send(2, pair(0, -1), -1)
            send(3, pair(1, 1), 1)

        def relay(send=send, arrived=arrived, pair=pair):
            send(4, pair(0, 1) + arrived(0), 1)
            send(5, pair(1, -1) + arrived(1), -1)

        def score(arrived=arrived, pair=pair):
            g = pair(0, 0) + arrived(2) + arrived(4)
            a = pair(1, 0) + arrived(3) + arrived(5)
            pairs[...] += g * a

        a1 = plan.task(far, 0.5, after=prev, arrivals=[to_core],
                       sends=[(m[0], "x1", size2), (m[1], "x-1", size2)], rank=rank)
        a2 = plan.task(near, 0.4, after=[a1], sends=[(m[2], "x-1", size2), (m[3], "x1", size2)], rank=rank)
        a3 = plan.task(relay, 0.6, after=[a2], arrivals=[m[0], m[1]], sends=[(m[4], "x1", size2), (m[5], "x-1", size2)], rank=rank)
        plan.task(score, 0.6, after=[a3], arrivals=[m[2], m[3], m[4], m[5]], rank=rank)

    for at in plan.order():
        plan.tasks[at][0]()

    used = plan.messages
    token = lax.broadcasted_iota(jnp.int32, (2, count), 1)
    first, both = lens[0], lens[0] + lens[1]
    summed = jnp.sum(pairs[...].reshape(2, each // 2, count), axis=1)
    by_example = [jnp.sum(jnp.where(mask, summed, 0.0), axis=1, keepdims=True)
                  for mask in (token < first, (token >= first) & (token < both))]
    factor = 1.0 / math.sqrt(LMAX * RANK)
    row = lax.broadcasted_iota(jnp.int32, (8, 128), 0)
    lane = lax.broadcasted_iota(jnp.int32, (8, 128), 1)
    score_of = jnp.where(row == 0, jnp.where(lane == 0, by_example[0][0:1], by_example[0][1:2]),
                         jnp.where(lane == 0, by_example[1][0:1], by_example[1][1:2]))
    named = jnp.where(row == 0, dest[0], jnp.where(row == 1, dest[1], -1)).astype(F32)
    exbuf[0] = jnp.where(lane == 2, named, score_of * factor)
    hops = lambda i: min(i // NZ, NY - i // NZ) + min(i % NZ, NZ - i % NZ)
    order = sorted(range(1, NY * NZ), key=lambda i: (-hops(i), i))
    fan(used, [(exbuf.at[0], exbuf.at[i], yz(i // NZ, i % NZ)) for i in order], group(exbuf.at[1 : NY * NZ]))
    landed(used, exbuf.at[1 : NY * NZ])
    every = exbuf[...].reshape(NY * NZ * 8, 128)
    target = every[:, 2:3]
    picked = [jnp.sum(jnp.where(target == (2 * ex + r).astype(F32), every, 0.0), axis=0, keepdims=True)[:, 0:2] for r in range(2)]
    out[...] = jnp.where(lax.broadcasted_iota(jnp.int32, (2, 2), 0) == 0, picked[0], picked[1])

    for one in sent:
        one.wait_send()


def shards(acts, grads, act_basis, grad_basis, act_query, grad_query, lengths, destination):
    grads, act_basis, grad_basis = grads.T, act_basis.T, grad_basis.T
    count, na = acts.shape
    nf = grads.shape[0]
    columns = grad_query.shape[1]
    chunks = columns // W
    tiles = -(-nf // 128) + -(-na // 128)
    lanes = -(-tiles // NY) * NY * 128
    short, wide = W // NZ, lanes // NY
    any_ = pl.BlockSpec(memory_space=pl.ANY)
    smem = pl.BlockSpec(memory_space=pltpu.SMEM)
    messages, groups = 2 + chunks * 23 + 2, 4 + chunks * 6
    return pl.pallas_call(
        kernel,
        out_shape=jax.ShapeDtypeStruct((2, 2), F32),
        in_specs=[smem, smem] + [any_] * 6,
        out_specs=pl.BlockSpec(memory_space=pltpu.VMEM),
        scratch_shapes=[
            pltpu.VMEM(acts.shape, BF16),
            pltpu.VMEM(grads.shape, BF16),
            pltpu.VMEM(act_basis.shape, BF16),
            pltpu.VMEM(grad_basis.shape, BF16),
            pltpu.VMEM(act_query.shape, BF16),
            pltpu.VMEM(grad_query.shape, BF16),
            pltpu.VMEM(act_query.shape[::-1], BF16),
            pltpu.VMEM(grad_query.shape[::-1], BF16),
            pltpu.VMEM((chunks, W, lanes), F32),
            pltpu.VMEM((chunks, W, lanes), BF16),
            pltpu.VMEM((chunks, 2, 3, W // 2, wide), I16),
            pltpu.VMEM((chunks, 2, 3, W // 2, wide), I16),
            pltpu.VMEM((chunks, W, wide), F32),
            pltpu.VMEM((chunks, W, wide), I16),
            pltpu.VMEM((chunks, NZ, short, wide), I16),
            pltpu.VMEM((chunks, 3, short, wide), I16),
            pltpu.VMEM((NY, 8, 128), F32),
            pltpu.VMEM((NZ, 8, 128), F32),
            pltpu.VMEM((chunks, 2, W, count), F32),
            pltpu.VMEM((chunks, 2, W // 2, count), F32),
            pltpu.VMEM((chunks, 6, W // (2 * NX), count + 128), I16),
            pltpu.VMEM((chunks, 6, W // (2 * NX), count + 128), I16),
            pltpu.VMEM((W // (2 * NX), count), F32),
            pltpu.VMEM((NY * NZ, 8, 128), F32),
            pltpu.SemaphoreType.DMA((6,)),
            pltpu.SemaphoreType.DMA((groups,)),
            pltpu.SemaphoreType.DMA((messages,)),
        ],
        compiler_params=pltpu.CompilerParams(collective_id=0, has_side_effects=True, vmem_limit_bytes=60 << 20),
        name="influence",
    )(lengths, destination, acts, grads, act_basis, grad_basis, act_query, grad_query)


def solution(mesh):
    return jax.shard_map(
        shards,
        mesh=mesh,
        in_specs=(
            P("ex", "lay"),
            P("ex", "lay"),
            P("lay", "ex"),
            P("lay", "ex"),
            P("ex", None),
            P("ex", None),
            P("ex"),
            P("ex"),
        ),
        out_specs=P("ex", "lay"),
        check_vma=False,
    )
```

```python
import functools
import math

import jax
import jax.numpy as jnp
from jax import lax
from jax.experimental import pallas as pl
from jax.experimental.pallas import tpu as pltpu
from jax.sharding import PartitionSpec as P

RANK = 32
LMAX = 1024
NY, NZ, NX = 4, 8, 4
W = 128
MESH = pl.DeviceIdType.MESH
F32, BF16 = jnp.float32, jnp.bfloat16


class Plan:
    def __init__(self):
        self.tasks = []
        self.messages = 0
        self.groups = 0

    def message(self, count=1):
        first = self.messages
        self.messages += count
        return first

    def group(self):
        self.groups += 1
        return self.groups - 1

    def task(self, emit, cost, after=(), arrivals=(), sends=(), rank=0):
        self.tasks.append((emit, cost, tuple(after), tuple(arrivals), tuple(sends), rank))
        return len(self.tasks) - 1

    def levels(self):
        level = [0.0] * len(self.tasks)
        users = [[] for _ in self.tasks]
        waits = {}
        for at, (_, _, after, arrivals, _, _) in enumerate(self.tasks):
            for a in after:
                users[a].append(at)
            for m in arrivals:
                waits.setdefault(m, []).append(at)
        for _ in range(len(self.tasks)):
            changed = False
            for at in reversed(range(len(self.tasks))):
                _, cost, _, _, sends, _ = self.tasks[at]
                best = max([level[u] for u in users[at]], default=0.0)
                for number, link, size in sends:
                    flight = 2.2 + size / 0.05 * 1e-3 if link != "core" else 1.0 + size / 0.3 * 1e-3
                    best = max([best] + [flight + level[u] for u in waits.get(number, [])])
                if cost + best > level[at] + 1e-9:
                    level[at] = cost + best
                    changed = True
            if not changed:
                break
        return level

    def order(self):
        now, done, arrived, link_free, left, out = 0.0, {}, {}, {}, list(range(len(self.tasks))), []
        level = self.levels()
        while left:
            best = None
            for at in left:
                _, cost, after, arrivals, _, rank = self.tasks[at]
                if any(a not in done for a in after) or any(m not in arrived for m in arrivals):
                    continue
                start = max([now] + [arrived[m] for m in arrivals])
                key = (start, -level[at], at)
                if best is None or key < best:
                    best = key
            start, _, at = best
            _, cost, _, _, sends, _ = self.tasks[at]
            now = start + cost
            done[at] = now
            for number, link, size in sends:
                rate, latency = (0.3, 2.5) if link == "core" else (0.045, 4.0 if link[0] == "x" else 2.2)
                begin = max(now, link_free.get(link, 0.0))
                link_free[link] = begin + size / rate * 1e-3
                arrived[number] = link_free[link] + latency
            left.remove(at)
            out.append(at)
        return out


I16 = jnp.int16
TOP = 32000.0


def encode(value, scale):
    return jnp.floor(value * scale + 0.5).astype(jnp.int32).astype(I16)


def decode(code, unit):
    return code.astype(jnp.int32).astype(F32) * unit


def kernel(lens, dest, acts, grads, abasis, gbasis, aquery, gquery, out,
           xa, xg, ba, bg, qa, qg, qat, qgt, part, fin, ysend, ybuf, acc, zsend, zbuf, relayed, hy, hz, pfull, precv,
           xs, xr, pairs, exbuf, ins, ss, rs):
    ex, lay = lax.axis_index("ex"), lax.axis_index("lay")
    y, z = lax.div(ex, NZ), lax.rem(ex, NZ)
    x, c = lax.div(lay, 2), lax.rem(lay, 2)
    nf, na = gbasis.shape[1], abasis.shape[1]
    base = -(-nf // 128) * 128
    chunks, _, lanes = part.shape
    count = acts.shape[0]
    tile = count // 8
    own = W // 2
    each = own // NX
    wide = lanes // NY
    short = W // NZ
    rows = W // 2

    def wrap(v, n):
        return lax.rem(v + n, n)

    def yz(dy, dz):
        return (wrap(y + dy, NY) * NZ + wrap(z + dz, NZ), lay)

    def across(dx, dc=0):
        return (ex, wrap(x + dx, NX) * 2 + wrap(c + dc, 2))

    def copy(number, src, dst, device, group=0):
        return pltpu.make_async_remote_copy(src, dst, ss.at[group], rs.at[number], device_id=device, device_id_type=MESH)

    loads = [(gquery, qg), (gbasis, bg), (aquery, qa), (abasis, ba), (grads, xg), (acts, xa)]
    local = [pltpu.make_async_copy(src, dst, ins.at[i]) for i, (src, dst) in enumerate(loads)]

    barrier = pltpu.get_barrier_semaphore()
    partners = [yz(0, 1), yz(0, -1), yz(1, 0), yz(-1, 0), across(1), across(-1), across(0, 1)]
    partners += [yz(2, 0)] + [yz(0, i) for i in range(2, NZ - 1)]
    for device in partners:
        pl.semaphore_signal(barrier, inc=1, device_id=device, device_id_type=MESH)
    for one in local:
        one.start()

    plan = Plan()
    sent = []

    def group(whole):
        number = plan.group()
        sent.append(copy(0, whole, whole, yz(0, 1), number))
        return number

    def post(number, src, dst, device, of):
        copy(number, src, dst, device, of).start()

    def fan(number, sends, of):
        for src, dst, device in sends:
            copy(number, src, dst, device, of).start()

    def landed(number, whole):
        copy(number, whole, whole, yz(0, 1)).wait_recv()

    def block(ref, row, height, lane, size):
        return ref.at[pl.ds(pl.multiple_of(row, 16), height), pl.ds(pl.multiple_of(lane, 128), size)]

    def piece(j, h, d):
        return block(part.at[j], h * rows, rows, d * wide, wide)

    def bounds(tile):
        return tile[0:1, 0:1], tile[0:1, 64:65]

    def spread(pair, d):
        lane = d * wide + lax.broadcasted_iota(jnp.int32, (1, wide), 1)
        return jnp.where(lane < base, pair[0], pair[1])

    def arrange(rows_of):
        out_rows = []
        for j in range(chunks):
            for core in range(2):
                for at in range(NX):
                    for q in (4 * at + 2 * core, 4 * at + 2 * core + 1):
                        out_rows.append(rows_of[q * RANK + 8 * j : q * RANK + 8 * j + 8])
        return jnp.concatenate(out_rows, axis=0).astype(BF16)

    hny, hnz = plan.message(), plan.message()
    state = {}

    def rot():
        local[0].wait()
        qgt[...] = arrange(qg[...].astype(F32).T)
        local[2].wait()
        qat[...] = arrange(qa[...].astype(F32).T)
        local[1].wait()
        largest = []
        for basis, query, size, at in ((bg, qgt, nf, 0), (ba, qat, na, base)):
            if size == na:
                local[3].wait()
            peak = jnp.zeros((1, 256), F32)
            for lo in range(0, size, 256):
                hi = min(lo + 256, size)
                r = jnp.dot(query[...], basis[:, lo:hi], preferred_element_type=F32)
                for j in range(chunks):
                    part[j, :, at + lo : at + hi] = r[j * W : (j + 1) * W]
                here = jnp.max(jnp.abs(r), axis=0, keepdims=True)
                if hi - lo < 256:
                    largest.append(jnp.max(here, axis=1, keepdims=True))
                else:
                    peak = jnp.maximum(peak, here)
            largest.append(jnp.max(peak, axis=1, keepdims=True))
        top_g, top_a = jnp.maximum(largest[0], largest[1]), jnp.maximum(largest[2], largest[3])
        for j in range(chunks):
            part[j, :, nf:base] = jnp.zeros((W, base - nf), F32)
            part[j, :, base + na :] = jnp.zeros((W, lanes - base - na), F32)
        lane = lax.broadcasted_iota(jnp.int32, (8, 128), 1)
        hy[0] = jnp.maximum(jnp.where(lane < 64, top_g, top_a), 1e-30)
        state["first"] = [TOP / b for b in bounds(hy[0])]
        pl.semaphore_wait(barrier, len(partners))
        fan(hny, [(hy.at[0], hy.at[i], yz(i, 0)) for i in range(1, NY)], group(hy.at[1:NY]))

    def scale_y():
        landed(hny, hy.at[1:NY])
        hz[0] = hy[0] + hy[1] + hy[2] + hy[3]
        for i in (1, 3):
            state["y", i] = [b * (1.0 / TOP) for b in bounds(hy[i])]
        fan(hnz, [(hz.at[0], hz.at[i], yz(0, i)) for i in range(1, NZ)], group(hz.at[1:NZ]))
        state["unit"] = [b * (1.0 / TOP) for b in bounds(hz[0])]
        state["scale"] = [TOP / b for b in bounds(hz[0])]

    def scale_z():
        landed(hnz, hz.at[1:NZ])
        for turn in (1, -1):
            for mine, over in ((0, turn), (0, -turn)):
                total = hz[0] + hz[over % NZ]
                state["two", over % NZ] = [TOP / b for b in bounds(total)]
            for k in (1, 3, -2):
                total = hz[turn * k % NZ] + hz[turn * (k + (1 if k > 0 else -1)) % NZ]
                state["sum", turn * k % NZ] = [b * (1.0 / TOP) for b in bounds(total)]
            state["z", turn % NZ] = [b * (1.0 / TOP) for b in bounds(hz[turn % NZ])]

    begin = plan.task(rot, 4.0, sends=[(hny, "y0", 0.0)])
    scaled = plan.task(scale_y, 0.3, after=[begin], arrivals=[hny], sends=[(hnz, "zz", 0.0)], rank=-1)
    begin2 = plan.task(scale_z, 0.3, after=[scaled], arrivals=[hnz], rank=-1)
    chain = {"t0": [begin], "t1": [], "t2": []}

    ready = []
    for j in range(chunks):
        rank = j
        size = rows * wide * 2e-3
        signs = (1, -1)
        n = [[plan.message() for _ in range(3)] for _ in signs]
        gy, gz, gz2, gy2 = group(ysend.at[j]), group(zbuf.at[j, 1:NZ]), group(zbuf.at[j, 1:NZ]), group(ysend.at[j])
        turn = 1 if j % 2 == 0 else -1

        def rs0(j=j, n=n, gy=gy):
            for h, sg in enumerate(signs):
                d = wrap(y + 2 * sg, NY)
                ysend[j, h, 0] = encode(piece(j, h, d)[...], spread(state["first"], d))
                post(n[h][0], ysend.at[j, h, 0], ybuf.at[j, h, 0], yz(sg, 0), gy)

        def rs1(j=j, n=n, gy=gy):
            for h, sg in enumerate(signs):
                d = wrap(y - sg, NY)
                ysend[j, h, 2] = encode(piece(j, h, d)[...], spread(state["first"], d))
                post(n[h][2], ysend.at[j, h, 2], ybuf.at[j, h, 2], yz(-sg, 0), gy)

        def rs2(h, sg, j=j, n=n, gy=gy):
            d = wrap(y + sg, NY)
            landed(n[h][0], ybuf.at[j, h, 0])
            total = piece(j, h, d)[...] + decode(ybuf[j, h, 0], spread(state["y", sg % NY], d))
            ysend[j, h, 1] = encode(total, spread(state["scale"], d))
            post(n[h][1], ysend.at[j, h, 1], ybuf.at[j, h, 1], yz(sg, 0), gy)

        zn = [plan.message() for _ in range(4)]

        def zrows(ref, step, j=j):
            return block(ref.at[j], wrap(z + step, NZ) * short, short, 0, wide)

        def middle(j=j, n=n, zn=zn, gz=gz, t=turn, zrows=zrows):
            unit, scale = spread(state["unit"], y), spread(state["scale"], y)
            other = [spread(state["y", -sg % NY], y) for sg in signs]
            for h in (0, 1):
                landed(n[h][1], ybuf.at[j, h, 1])
                landed(n[h][2], ybuf.at[j, h, 2])
                total = piece(j, h, y)[...] + decode(ybuf[j, h, 1], unit) + decode(ybuf[j, h, 2], other[h])
                acc[j, h * rows : (h + 1) * rows, :] = total
                zsend[j, h * rows : (h + 1) * rows, :] = encode(total, scale)
            fan(zn[0], [(zrows(zsend, 4), zbuf.at[j, 0], yz(0, t)), (zrows(zsend, 2 * t), zbuf.at[j, 1], yz(0, t)),
                        (zrows(zsend, -3 * t), zbuf.at[j, 2], yz(0, -t))], gz)
            fan(zn[1], [(zrows(zsend, -t), zbuf.at[j, 3], yz(0, -t))], gz)

        def relay_z(j=j, zn=zn, gz=gz, t=turn, zrows=zrows):
            landed(zn[0], zbuf.at[j, 0:3])
            near = spread(state["z", t % NZ], y)
            far = spread(state["z", -t % NZ], y)
            ahead, back = spread(state["two", t % NZ], y), spread(state["two", -t % NZ], y)
            for k, (got, step, unit, scale) in enumerate(((0, 3 * t, near, ahead), (1, t, near, ahead), (2, -2 * t, far, back))):
                relayed[j, k] = encode(zrows(acc, step)[...] + decode(zbuf[j, got], unit), scale)
            fan(zn[1], [(relayed.at[j, k], zbuf.at[j, 4 + k], yz(0, step)) for k, step in ((0, 3 * t), (1, t), (2, -2 * t))], gz)

        def finish(j=j, zn=zn, gz2=gz2, t=turn, zrows=zrows):
            landed(zn[1], zbuf.at[j, 3:7])
            total = zrows(acc, 0)[...] + decode(zbuf[j, 3], spread(state["z", -t % NZ], y))
            for k, step in ((4, 3 * t), (5, t), (6, -2 * t)):
                total = total + decode(zbuf[j, k], spread(state["sum", step % NZ], y))
            mine = block(fin.at[j], z * short, short, y * wide, wide)
            mine[...] = total.astype(BF16)
            fan(zn[2], [(mine, mine, yz(0, step)) for step in (3 * t, t, -t, -2 * t)], gz2)

        def spread_z(j=j, zn=zn, gz2=gz2, t=turn):
            landed(zn[2], zbuf.at[j, 0:4])
            for step, to in ((-3 * t, t), (-t, t), (2 * t, -t)):
                got = block(fin.at[j], wrap(z + step, NZ) * short, short, y * wide, wide)
                fan(zn[3], [(got, got, yz(0, to))], gz2)

        a = [plan.message() for _ in range(6)]

        def fin_half(j, h, d):
            return block(fin.at[j], h * rows, rows, d * wide, wide)

        def ag0(zn=zn, a=a, j=j, gy2=gy2):
            landed(zn[3], zbuf.at[j, 0:3])
            for h, sg in enumerate(signs):
                mine = fin_half(j, h, y)
                post(a[3 * h], mine, mine, yz(sg, 0), gy2)
            for h, sg in enumerate(signs):
                mine = fin_half(j, h, y)
                post(a[3 * h + 2], mine, mine, yz(-sg, 0), gy2)

        def ag1(h, sg, a=a, j=j, gy2=gy2):
            got = fin_half(j, h, wrap(y - sg, NY))
            landed(a[3 * h], got)
            post(a[3 * h + 1], got, got, yz(sg, 0), gy2)

        def complete(a=a, j=j):
            for h, sg in enumerate(signs):
                landed(a[3 * h + 1], fin_half(j, h, wrap(y - 2 * sg, NY)))
                landed(a[3 * h + 2], fin_half(j, h, wrap(y + sg, NY)))
            if j == 0:
                for one in local[4:]:
                    one.wait()

        t0 = plan.task(rs0, 0.3, after=chain["t0"], sends=[(n[0][0], "y1", size), (n[1][0], "y-1", size)], rank=rank)
        t1 = plan.task(rs1, 0.3, after=chain["t1"] + [t0], sends=[(n[0][2], "y-1", size), (n[1][2], "y1", size)], rank=rank)
        t2 = []
        for h, sg in enumerate(signs):
            def rs2_of(h=h, sg=sg, rs2=rs2):
                rs2(h, sg)

            rs2_of.__name__ = "rs2"
            t2.append(plan.task(rs2_of, 0.3, after=[t0, scaled], arrivals=[n[h][0]], sends=[(n[h][1], "y%d" % sg, size)], rank=rank))
        chain["t0"], chain["t1"] = [t1] if j == 0 else chain["t2"], t2
        chain["t2"] = t2
        unit_z = short * wide * 2e-3
        t3 = plan.task(middle, 0.6, after=t2 + [t1], arrivals=[n[0][1], n[0][2], n[1][1], n[1][2]],
                       sends=[(zn[0], "z%d" % turn, 2 * unit_z), (zn[1], "z%d" % -turn, 2 * unit_z)], rank=rank)
        t3 = plan.task(relay_z, 0.3, after=[t3, begin2], arrivals=[zn[0]],
                       sends=[(zn[1], "z%d" % turn, 4 * unit_z), (n[0][0], "z%d" % -turn, 2 * unit_z)], rank=rank)
        t4 = plan.task(finish, 0.3, after=[t3], arrivals=[zn[1]],
                       sends=[(zn[2], "z%d" % turn, 4 * unit_z), (n[0][0], "z%d" % -turn, 3 * unit_z)], rank=rank)
        t4 = plan.task(spread_z, 0.1, after=[t4], arrivals=[zn[2]],
                       sends=[(zn[3], "z%d" % turn, 2 * unit_z), (n[0][0], "z%d" % -turn, unit_z)], rank=rank)
        t5 = plan.task(ag0, 0.2, after=[t4], arrivals=[zn[3]], sends=[(a[0], "y1", size), (a[3], "y-1", size), (a[2], "y-1", size), (a[5], "y1", size)], rank=rank)
        t6 = []
        for h, sg in enumerate(signs):
            def ag1_of(h=h, sg=sg, ag1=ag1):
                ag1(h, sg)

            ag1_of.__name__ = "ag1"
            t6.append(plan.task(ag1_of, 0.1, after=[t5], arrivals=[a[3 * h]], sends=[(a[3 * h + 1], "y%d" % sg, size)], rank=rank))
        ready.append(plan.task(complete, 0.1, after=t6, arrivals=[a[1], a[2], a[4], a[5]], rank=rank))

    size4 = 4 * tile * own * 4e-3
    size2 = each * (count + 128) * 2e-3
    pairs[...] = jnp.zeros(pairs.shape, F32)
    log2 = 1.0 / math.log(2.0)

    def pack(dst, value):
        bound = jnp.maximum(jnp.max(jnp.max(jnp.abs(value), axis=0, keepdims=True), axis=1, keepdims=True), 1e-30)
        power = jnp.ceil(jnp.log(bound) * log2)
        dst[:, :count] = encode(value, TOP * jnp.exp(power * (-1.0 / log2)))
        dst[:, count:] = jnp.broadcast_to(power, (each, 128)).astype(jnp.int32).astype(I16)

    def unpack(src):
        power = src[:, count:].astype(jnp.int32).astype(F32)[0:1, 0:1]
        return decode(src[:, :count], jnp.exp(power * (1.0 / log2)) * (1.0 / TOP))

    for j in range(chunks):
        rank = 10 + j
        to_core = plan.message()
        gc, gx = group(precv.at[j]), group(xs.at[j])

        def theirs_block(j, i):
            return pfull.at[j, :, pl.ds(pl.multiple_of((1 - c) * own, 16), own), 4 * i * tile : 4 * (i + 1) * tile]

        def there_block(j, i):
            return precv.at[j, :, :, 4 * i * tile : 4 * (i + 1) * tile]

        prev = [ready[j]]
        for i in range(8):
            def project(i=i, j=j, gc=gc, to_core=to_core, theirs_block=theirs_block, there_block=there_block):
                token = slice(i * tile, (i + 1) * tile)
                pfull[j, 0, :, token] = jnp.dot(fin[j, :, :nf], xg[:, token], preferred_element_type=F32)
                pfull[j, 1, :, token] = lax.dot_general(
                    fin[j, :, base : base + na], xa[token, :], (((1,), (1,)), ((), ())), preferred_element_type=F32)
                if i % 4 == 3:
                    post(to_core, theirs_block(j, i // 4), there_block(j, i // 4), across(0, 1), gc)

            prev = [plan.task(project, 0.27, after=prev, sends=[(to_core, "core", 2 * size4)] if i % 4 == 3 else [], rank=rank)]
        m = [plan.message() for _ in range(6)]

        def pair(k, dx, j=j):
            to = wrap(x + dx, NX) * each
            return (pfull[j, k, pl.ds(pl.multiple_of(c * own + to, 16), each), :]
                    + precv[j, k, pl.ds(pl.multiple_of(to, 16), each), :])

        def send(k, value, dx, j=j, m=m, gx=gx):
            pack(xs.at[j, k], value)
            post(m[k], xs.at[j, k], xr.at[j, k], across(dx), gx)

        def arrived(k, j=j, m=m):
            landed(m[k], xr.at[j, k])
            return unpack(xr.at[j, k])

        def far(j=j, send=send, pair=pair, to_core=to_core):
            landed(to_core, precv.at[j])
            send(0, pair(0, 2), 1)
            send(1, pair(1, 2), -1)

        def near(send=send, pair=pair):
            send(2, pair(0, -1), -1)
            send(3, pair(1, 1), 1)

        def relay(send=send, arrived=arrived, pair=pair):
            send(4, pair(0, 1) + arrived(0), 1)
            send(5, pair(1, -1) + arrived(1), -1)

        def score(arrived=arrived, pair=pair):
            g = pair(0, 0) + arrived(2) + arrived(4)
            a = pair(1, 0) + arrived(3) + arrived(5)
            pairs[...] += g * a

        a1 = plan.task(far, 0.5, after=prev, arrivals=[to_core],
                       sends=[(m[0], "x1", size2), (m[1], "x-1", size2)], rank=rank)
        a2 = plan.task(near, 0.4, after=[a1], sends=[(m[2], "x-1", size2), (m[3], "x1", size2)], rank=rank)
        a3 = plan.task(relay, 0.6, after=[a2], arrivals=[m[0], m[1]], sends=[(m[4], "x1", size2), (m[5], "x-1", size2)], rank=rank)
        plan.task(score, 0.6, after=[a3], arrivals=[m[2], m[3], m[4], m[5]], rank=rank)

    for at in plan.order():
        plan.tasks[at][0]()

    used = plan.messages
    token = lax.broadcasted_iota(jnp.int32, (2, count), 1)
    first, both = lens[0], lens[0] + lens[1]
    summed = jnp.sum(pairs[...].reshape(2, each // 2, count), axis=1)
    by_example = [jnp.sum(jnp.where(mask, summed, 0.0), axis=1, keepdims=True)
                  for mask in (token < first, (token >= first) & (token < both))]
    factor = 1.0 / math.sqrt(LMAX * RANK)
    row = lax.broadcasted_iota(jnp.int32, (8, 128), 0)
    lane = lax.broadcasted_iota(jnp.int32, (8, 128), 1)
    score_of = jnp.where(row == 0, jnp.where(lane == 0, by_example[0][0:1], by_example[0][1:2]),
                         jnp.where(lane == 0, by_example[1][0:1], by_example[1][1:2]))
    named = jnp.where(row == 0, dest[0], jnp.where(row == 1, dest[1], -1)).astype(F32)
    exbuf[0] = jnp.where(lane == 2, named, score_of * factor)
    hops = lambda i: min(i // NZ, NY - i // NZ) + min(i % NZ, NZ - i % NZ)
    order = sorted(range(1, NY * NZ), key=lambda i: (-hops(i), i))
    fan(used, [(exbuf.at[0], exbuf.at[i], yz(i // NZ, i % NZ)) for i in order], group(exbuf.at[1 : NY * NZ]))
    landed(used, exbuf.at[1 : NY * NZ])
    every = exbuf[...].reshape(NY * NZ * 8, 128)
    target = every[:, 2:3]
    picked = [jnp.sum(jnp.where(target == (2 * ex + r).astype(F32), every, 0.0), axis=0, keepdims=True)[:, 0:2] for r in range(2)]
    out[...] = jnp.where(lax.broadcasted_iota(jnp.int32, (2, 2), 0) == 0, picked[0], picked[1])

    for one in sent:
        one.wait_send()


def shards(acts, grads, act_basis, grad_basis, act_query, grad_query, lengths, destination):
    grads, act_basis, grad_basis = grads.T, act_basis.T, grad_basis.T
    count, na = acts.shape
    nf = grads.shape[0]
    columns = grad_query.shape[1]
    chunks = columns // W
    tiles = -(-nf // 128) + -(-na // 128)
    lanes = -(-tiles // NY) * NY * 128
    short, wide = W // NZ, lanes // NY
    any_ = pl.BlockSpec(memory_space=pl.ANY)
    smem = pl.BlockSpec(memory_space=pltpu.SMEM)
    messages, groups = 2 + chunks * 23 + 2, 4 + chunks * 6
    return pl.pallas_call(
        kernel,
        out_shape=jax.ShapeDtypeStruct((2, 2), F32),
        in_specs=[smem, smem] + [any_] * 6,
        out_specs=pl.BlockSpec(memory_space=pltpu.VMEM),
        scratch_shapes=[
            pltpu.VMEM(acts.shape, BF16),
            pltpu.VMEM(grads.shape, BF16),
            pltpu.VMEM(act_basis.shape, BF16),
            pltpu.VMEM(grad_basis.shape, BF16),
            pltpu.VMEM(act_query.shape, BF16),
            pltpu.VMEM(grad_query.shape, BF16),
            pltpu.VMEM(act_query.shape[::-1], BF16),
            pltpu.VMEM(grad_query.shape[::-1], BF16),
            pltpu.VMEM((chunks, W, lanes), F32),
            pltpu.VMEM((chunks, W, lanes), BF16),
            pltpu.VMEM((chunks, 2, 3, W // 2, wide), I16),
            pltpu.VMEM((chunks, 2, 3, W // 2, wide), I16),
            pltpu.VMEM((chunks, W, wide), F32),
            pltpu.VMEM((chunks, W, wide), I16),
            pltpu.VMEM((chunks, NZ, short, wide), I16),
            pltpu.VMEM((chunks, 3, short, wide), I16),
            pltpu.VMEM((NY, 8, 128), F32),
            pltpu.VMEM((NZ, 8, 128), F32),
            pltpu.VMEM((chunks, 2, W, count), F32),
            pltpu.VMEM((chunks, 2, W // 2, count), F32),
            pltpu.VMEM((chunks, 6, W // (2 * NX), count + 128), I16),
            pltpu.VMEM((chunks, 6, W // (2 * NX), count + 128), I16),
            pltpu.VMEM((W // (2 * NX), count), F32),
            pltpu.VMEM((NY * NZ, 8, 128), F32),
            pltpu.SemaphoreType.DMA((6,)),
            pltpu.SemaphoreType.DMA((groups,)),
            pltpu.SemaphoreType.DMA((messages,)),
        ],
        compiler_params=pltpu.CompilerParams(collective_id=0, has_side_effects=True, vmem_limit_bytes=60 << 20),
        name="influence",
    )(lengths, destination, acts, grads, act_basis, grad_basis, act_query, grad_query)


def solution(mesh):
    return jax.shard_map(
        shards,
        mesh=mesh,
        in_specs=(
            P("ex", "lay"),
            P("ex", "lay"),
            P("lay", "ex"),
            P("lay", "ex"),
            P("ex", None),
            P("ex", None),
            P("ex"),
            P("ex"),
        ),
        out_specs=P("ex", "lay"),
        check_vma=False,
    )
```
